32 devices in a mesh: dp: 8 (over z, y), sp: 4 (over x, core).
Axes of the slice: x: 2, y: 2, z: 4, core: 2. Of those that a mesh axis runs over, the one named last changes fastest.
Arguments:
- queries: bfloat16 [4096, 2560], P(('dp', 'sp')), may hold values from -80 to 80
- key_rows: bfloat16 [4096, 2560], P(('dp', 'sp')), may hold values from -5 to 5
- value_rows: bfloat16 [4096, 2560], P(('dp', 'sp')), may hold values from -6 to 6
- cotangent: bfloat16 [4096, 2560], P(('dp', 'sp')), may hold values from -6 to 6
- lengths: int32 [8], replicated, may hold values from 1 to 512, 2560 in all
- sample_plan: int32 [8], replicated, may hold values from 0 to 7, each once
- guide_bins: int32 [8], replicated, may hold values from 0 to 7
- guide_table: float32 [8, 20], replicated, may hold values from 0.5 to 2
- block_source: int32 [1024], replicated, may hold values from 0 to 1023, as said below
Outputs:
- attn_out: bfloat16 [4096, 2560], P(('dp', 'sp'))
- grad_queries: bfloat16 [4096, 2560], P(('dp', 'sp'))
- grad_keys: bfloat16 [4096, 2560], P(('dp', 'sp'))
- grad_values: bfloat16 [4096, 2560], P(('dp', 'sp'))
The draws below stay inside these ranges and needn't reach their ends.
Inputs may be any that keep to these rules, and one draw needn't show every extreme that they name: `lengths`: the longest sample has exactly 512 tokens. `sample_plan`: every group takes exactly one sample. `block_source`: a permutation; the 32 row blocks of the group order that one device holds come one from each device's loader rows, and each device's 32 loader row blocks go one to each device.
All inputs are finite; a program needn't handle non-finite values.
Results may differ from the reference program's by a relative error of at most 0.009.
Values may be sent and summed in bfloat16 or wider, within the bound.
A program may use at most 64 MiB of HBM per device.

```python
import math
import jax
import jax.numpy as jnp
import numpy as np
from jax import lax

HEADS = 20
HD = 128
BINS = 8
LOADERS = 32
GROUP_TOK = 512
TOKENS = 4096
BLK = 4
NBLK = 1024
N_DP = 8


def shared_rows(key):
    base = jnp.clip(jax.random.normal(jax.random.fold_in(key, 5), (TOKENS, HEADS * HD), jnp.float32), -5.0, 5.0)
    picked = jax.random.randint(jax.random.fold_in(key, 6), (TOKENS,), 0, 8) == 0
    strength = 10.0 * jax.random.randint(jax.random.fold_in(key, 7), (TOKENS, 1), 1, 4).astype(jnp.float32)
    return (base, picked, strength)


def draw_key_rows(key, part):
    base, picked, strength = shared_rows(key)
    key = jax.random.fold_in(key, 21)
    row_ids = jnp.arange(TOKENS, dtype=jnp.int32)
    offset = row_ids % BLK
    first_row = row_ids - offset
    spread = jax.random.uniform(key, (TOKENS, 1), jnp.float32, 1.5, 2.5)
    ripple = spread / (strength[first_row] * math.sqrt(HD))
    paired = (offset == 1) & picked[first_row]
    moved = jnp.clip(base[first_row] * (1.0 + ripple), -5.0, 5.0)
    values = jnp.where(paired[:, None], moved, base)
    return values.astype(jnp.bfloat16)


def draw_queries(key, part):
    base, picked, strength = shared_rows(key)
    key = jax.random.fold_in(key, 22)
    row_ids = jnp.arange(TOKENS, dtype=jnp.int32)
    offset = row_ids % BLK
    fresh = jnp.clip(jax.random.normal(key, (TOKENS, HEADS * HD), jnp.float32), -5.0, 5.0)
    aligned = (offset == 0) & picked
    strong = jnp.clip(strength * base, -80.0, 80.0)
    values = jnp.where(aligned[:, None], strong, fresh)
    return values.astype(jnp.bfloat16)


def draw_block_source(key, part):
    key = jax.random.fold_in(key, 23)
    owner_keys = jax.random.split(jax.random.fold_in(key, 1), LOADERS)
    loader_keys = jax.random.split(jax.random.fold_in(key, 2), LOADERS)
    sigma = jax.vmap(lambda sub_key: jax.random.permutation(sub_key, LOADERS))(owner_keys)
    tau = jax.vmap(lambda sub_key: jax.random.permutation(sub_key, LOADERS))(loader_keys)
    owner_ids = jnp.arange(LOADERS, dtype=jnp.int32)[:, None]
    loader_slot = tau[sigma, owner_ids]
    return (sigma * LOADERS + loader_slot).astype(jnp.int32).reshape(NBLK)


def with_ends(values, stream_key, low, top_value):
    dims = values.shape
    index_at = [jax.random.randint(jax.random.fold_in(stream_key, axis), (), 0, dims[axis]) for axis in range(len(dims))]
    values = values.at[tuple(index_at)].set(low)
    longest = dims.index(max(dims))
    index_at[longest] = (index_at[longest] + 1) % dims[longest]
    return values.at[tuple(index_at)].set(top_value)


def level_of(stream_key, shape, pieces, smallest, high):
    gain, own = 1.0, jax.random.fold_in(stream_key, 6)
    for axis_at, blocks in pieces:
        steps = jnp.exp(jax.random.uniform(jax.random.fold_in(own, axis_at), (blocks,), jnp.float32, smallest / len(pieces), high / len(pieces)))
        gain = gain * jnp.repeat(steps, shape[axis_at] // blocks).reshape([-1 if axis == axis_at else 1 for axis in range(len(shape))])
    return gain


def length_profile(count, total, limit, slope):
    weights = [(1 << 20) // math.isqrt(rank ** slope) + 1 for rank in range(2, count + 1)]
    spare, given = total - limit - (count - 1), [1] * (count - 1)
    while spare > 0:
        free = [i for i in range(count - 1) if given[i] < limit]
        whole, budget = sum([weights[i] for i in free]), spare
        for i in free:
            addition = min(limit - given[i], max(1, budget * weights[i] // whole), spare)
            given[i] = given[i] + addition
            spare = spare - addition
    return np.array([limit] + given)


def ragged(rng, amount, total, reach, lean):
    if amount == 2:
        one = jax.random.randint(rng, (), max(1, total - reach), min(reach, total - 1) + 1)
        return jnp.stack([one, total - one])
    tallies = jnp.asarray(length_profile(amount, total, reach, lean), jnp.int32)
    couples = (amount - 1) // 2
    donor, receiver = tallies[1:1 + 2 * couples:2], tallies[2:2 + 2 * couples:2]
    slack = jnp.minimum(donor - 1, reach - receiver)
    moved = jax.random.randint(jax.random.fold_in(rng, 1), (couples,), 0, 1 << 20) % (slack + 1)
    tallies = tallies.at[1:1 + 2 * couples:2].set(donor - moved).at[2:2 + 2 * couples:2].set(receiver + moved)
    return tallies[jax.random.permutation(jax.random.fold_in(rng, 2), amount)]


def normal_values(own_key, extent, deviation, limit, cuts=(), held_as=jnp.bfloat16):
    gain = level_of(own_key, extent, cuts, -0.22, 0.18) if cuts else 1.0
    entries = jax.random.normal(own_key, extent, jnp.float32) * deviation * gain
    return jnp.minimum(jnp.maximum(entries, -limit), limit).astype(held_as)


def setup_inputs(seed: int = 0) -> dict:
    keys = jax.random.split(jax.random.key(seed), 10)
    queries = draw_queries(jax.random.fold_in(keys[9], 71), 0)
    key_rows = draw_key_rows(jax.random.fold_in(keys[9], 71), 0)
    value_rows = normal_values(keys[2], (TOKENS, HEADS * HD), 1.0, 6.0, ((0, 32),))
    cotangent = normal_values(keys[3], (TOKENS, HEADS * HD), 1.0, 6.0, ((0, 32),))
    lengths = ragged(keys[4], N_DP, N_DP * GROUP_TOK * 5 // 8, GROUP_TOK, 2).astype(jnp.int32)
    sample_plan = jax.random.permutation(keys[5], N_DP).astype(jnp.int32)
    guide_bins = with_ends(jax.random.randint(keys[6], (N_DP,), 0, BINS), jax.random.fold_in(keys[6], 1), 0, BINS - 1).astype(jnp.int32)
    guide_table = jnp.clip(jax.random.uniform(keys[7], (BINS, HEADS), jnp.float32, 0.5, 2.0), 0.5, 2.0)
    block_source = draw_block_source(jax.random.fold_in(keys[9], 71), 0)
    return {"queries": queries, "key_rows": key_rows, "value_rows": value_rows, "cotangent": cotangent, "lengths": lengths, "sample_plan": sample_plan, "guide_bins": guide_bins, "guide_table": guide_table, "block_source": block_source}


def head_pass(query_head, key_head, value_head, grad_head, query_live, key_live):
    scores = jnp.dot(query_head, key_head.T, preferred_element_type=jnp.float32) * (HD ** -0.5)
    masked = jnp.where(key_live[None, :], scores, -1e30)
    top_score = jnp.max(masked, axis=1, keepdims=True)
    shifted_exp = jnp.where(key_live[None, :], jnp.exp(masked - top_score), 0.0)
    row_total = jnp.sum(shifted_exp, axis=1, keepdims=True)
    attend = jnp.where(query_live[:, None], shifted_exp / row_total, 0.0)
    attend_bf = attend.astype(jnp.bfloat16)
    output = jnp.dot(attend_bf, value_head, preferred_element_type=jnp.float32)
    grad_attend = jnp.dot(grad_head, value_head.T, preferred_element_type=jnp.float32)
    row_dot = jnp.sum(grad_head.astype(jnp.float32) * output, axis=1, keepdims=True)
    grad_scores = (attend * (grad_attend - row_dot) * (HD ** -0.5)).astype(jnp.bfloat16)
    grad_query = jnp.dot(grad_scores, key_head, preferred_element_type=jnp.float32)
    grad_key = jnp.dot(grad_scores.T, query_head, preferred_element_type=jnp.float32)
    grad_value = jnp.dot(attend_bf.T, grad_head, preferred_element_type=jnp.float32)
    return output, grad_query, grad_key, grad_value


def reference(queries, key_rows, value_rows, cotangent, lengths, sample_plan, guide_bins, guide_table, block_source):
    row_width = HEADS * HD

    def owned(source):
        return source.reshape(NBLK, BLK, row_width)[block_source].reshape(N_DP, GROUP_TOK, HEADS, HD)

    group_len = jnp.zeros((N_DP,), jnp.int32).at[sample_plan].set(lengths)
    group_bin = jnp.zeros((N_DP,), jnp.int32).at[sample_plan].set(guide_bins)
    head_gates = guide_table[group_bin]
    grad_own = (head_gates[:, None, :, None] * cotangent.reshape(N_DP, GROUP_TOK, HEADS, HD).astype(jnp.float32)).astype(jnp.bfloat16)

    def group_pass(group_items):
        query_group, key_group, value_group, grad_group, length_group = group_items
        live_rows = jnp.arange(GROUP_TOK, dtype=jnp.int32) < length_group

        def one_head(head_items):
            results = head_pass(head_items[0], head_items[1], head_items[2], head_items[3], live_rows, live_rows)
            return tuple(result.astype(jnp.bfloat16) for result in results)

        stacked = tuple(jnp.moveaxis(source, 1, 0) for source in (query_group, key_group, value_group, grad_group))
        results = lax.map(one_head, stacked)
        return tuple(jnp.moveaxis(result, 0, 1) for result in results)

    out_bf, grad_q, grad_k, grad_v = lax.map(group_pass, (owned(queries), owned(key_rows), owned(value_rows), grad_own, group_len))
    attn_out = (head_gates[:, None, :, None] * lax.optimization_barrier(out_bf).astype(jnp.float32)).astype(jnp.bfloat16).reshape(TOKENS, row_width)

    def loader_layout(source):
        blocks = source.reshape(NBLK, BLK, row_width)
        return jnp.zeros((NBLK, BLK, row_width), jnp.bfloat16).at[block_source].set(blocks).reshape(TOKENS, row_width)

    return attn_out, loader_layout(grad_q), loader_layout(grad_k), loader_layout(grad_v)
```

```python
import functools

import jax
import jax.numpy as jnp
from jax import lax
from jax.experimental import pallas as pl
from jax.experimental.pallas import tpu as pltpu
from jax.sharding import PartitionSpec as P

HEADS = 20
HD = 128
MESH = pl.DeviceIdType.MESH
F32 = jnp.float32
BF16 = jnp.bfloat16


def head_pass(query_head, key_head, value_head, grad_head, query_live, key_live):
    scores = jnp.dot(query_head, key_head.T, preferred_element_type=jnp.float32) * HD ** (-0.5)
    masked = jnp.where(key_live[None, :], scores, -1e30)
    top_score = jnp.max(masked, axis=1, keepdims=True)
    shifted_exp = jnp.where(key_live[None, :], jnp.exp(masked - top_score), 0.0)
    row_total = jnp.sum(shifted_exp, axis=1, keepdims=True)
    attend = jnp.where(query_live[:, None], shifted_exp / row_total, 0.0)
    attend_bf = attend.astype(jnp.bfloat16)
    output = jnp.dot(attend_bf, value_head, preferred_element_type=jnp.float32)
    grad_attend = jnp.dot(grad_head, value_head.T, preferred_element_type=jnp.float32)
    row_dot = jnp.sum(grad_head.astype(jnp.float32) * output, axis=1, keepdims=True)
    grad_scores = (attend * (grad_attend - row_dot) * HD ** (-0.5)).astype(jnp.bfloat16)
    grad_query = jnp.dot(grad_scores, key_head, preferred_element_type=jnp.float32)
    grad_key = jnp.dot(grad_scores.T, query_head, preferred_element_type=jnp.float32)
    grad_value = jnp.dot(attend_bf.T, grad_head, preferred_element_type=jnp.float32)
    return (output, grad_query, grad_key, grad_value)


def head_stack(query_part, key_part, value_part, grad_part, query_live, key_live):

    def one_head(head_items):
        return head_pass(
            head_items[0], head_items[1], head_items[2], head_items[3], query_live, key_live
        )

    stacked = tuple(
        (jnp.moveaxis(source, 1, 0) for source in (query_part, key_part, value_part, grad_part))
    )
    return lax.map(one_head, stacked)


def dispatch(first, second, third):
    return (
        lax.all_to_all(first, ("dp", "sp"), split_axis=0, concat_axis=0, tiled=True),
        lax.all_to_all(second, ("dp", "sp"), split_axis=0, concat_axis=0, tiled=True),
        lax.all_to_all(third, ("dp", "sp"), split_axis=0, concat_axis=0, tiled=True),
    )


def send_back(first, second, third):
    return (
        lax.all_to_all(first, ("dp", "sp"), split_axis=0, concat_axis=0, tiled=True),
        lax.all_to_all(second, ("dp", "sp"), split_axis=0, concat_axis=0, tiled=True),
        lax.all_to_all(third, ("dp", "sp"), split_axis=0, concat_axis=0, tiled=True),
    )


def per_device(
    queries,
    key_rows,
    value_rows,
    cotangent,
    lengths,
    sample_plan,
    guide_bins,
    guide_table,
    block_source,
):
    n_dp = lax.axis_size("dp")
    n_sp = lax.axis_size("sp")
    loaders = n_dp * n_sp
    tok_rows = queries.shape[0]
    row_width = queries.shape[1]
    block_rows = tok_rows // loaders
    device_index = lax.axis_index("dp") * n_sp + lax.axis_index("sp")
    table = block_source.reshape(loaders, loaders)
    sources = table[device_index] // loaders
    send_slot = jnp.sum(jnp.where(table // loaders == device_index, table % loaders, 0), axis=1)
    slot_index = jnp.arange(loaders, dtype=jnp.int32)
    back_slot = jnp.sum(
        jnp.where(sources[None, :] == slot_index[:, None], slot_index[None, :], 0), axis=1
    )
    loader_slot = jnp.sum(
        jnp.where(send_slot[None, :] == slot_index[:, None], slot_index[None, :], 0), axis=1
    )

    def as_blocks(source, order):
        return source.reshape(loaders, block_rows, row_width)[order]

    recv_query, recv_key, recv_value = dispatch(
        as_blocks(queries, send_slot),
        as_blocks(key_rows, send_slot),
        as_blocks(value_rows, send_slot),
    )
    query_own = recv_query[sources].reshape(tok_rows, HEADS, HD)
    key_own = recv_key[sources].reshape(tok_rows, HEADS, HD)
    value_own = recv_value[sources].reshape(tok_rows, HEADS, HD)
    group_index = lax.axis_index("dp")
    picked = sample_plan == group_index
    group_len = jnp.sum(jnp.where(picked, lengths, 0))
    group_bin = jnp.sum(jnp.where(picked, guide_bins, 0))
    bin_match = jnp.arange(guide_table.shape[0], dtype=jnp.int32) == group_bin
    head_gate = jnp.sum(jnp.where(bin_match[:, None], guide_table, 0.0), axis=0)
    grad_own = (
        head_gate[None, :, None] * cotangent.reshape(tok_rows, HEADS, HD).astype(jnp.float32)
    ).astype(jnp.bfloat16)
    heads_dev = HEADS // n_sp
    split_shape = (tok_rows, n_sp, heads_dev, HD)
    group_items = (
        lax.all_to_all(
            query_own.reshape(split_shape), "sp", split_axis=1, concat_axis=0, tiled=True
        ),
        lax.all_to_all(key_own.reshape(split_shape), "sp", split_axis=1, concat_axis=0, tiled=True),
        lax.all_to_all(
            value_own.reshape(split_shape), "sp", split_axis=1, concat_axis=0, tiled=True
        ),
        lax.all_to_all(
            grad_own.reshape(split_shape), "sp", split_axis=1, concat_axis=0, tiled=True
        ),
    )
    flat_items = tuple((item[:, 0] for item in group_items))
    live_rows = jnp.arange(flat_items[0].shape[0], dtype=jnp.int32) < group_len
    results = head_stack(
        flat_items[0], flat_items[1], flat_items[2], flat_items[3], live_rows, live_rows
    )
    out_heads, gq_heads, gk_heads, gv_heads = tuple(
        (jnp.moveaxis(result, 0, 1)[:, None].astype(jnp.bfloat16) for result in results)
    )
    back_rows = (
        lax.all_to_all(out_heads, "sp", split_axis=0, concat_axis=1, tiled=True),
        lax.all_to_all(gq_heads, "sp", split_axis=0, concat_axis=1, tiled=True),
        lax.all_to_all(gk_heads, "sp", split_axis=0, concat_axis=1, tiled=True),
        lax.all_to_all(gv_heads, "sp", split_axis=0, concat_axis=1, tiled=True),
    )
    out_bf, grad_q_own, grad_k_own, grad_v_own = tuple(
        (part.reshape(tok_rows, HEADS, HD) for part in back_rows)
    )
    attn_out = (
        (head_gate[None, :, None] * lax.optimization_barrier(out_bf).astype(jnp.float32))
        .astype(jnp.bfloat16)
        .reshape(tok_rows, row_width)
    )
    back_query, back_key, back_value = send_back(
        as_blocks(grad_q_own, back_slot),
        as_blocks(grad_k_own, back_slot),
        as_blocks(grad_v_own, back_slot),
    )
    grad_queries = back_query[loader_slot].reshape(tok_rows, row_width)
    grad_keys = back_key[loader_slot].reshape(tok_rows, row_width)
    grad_values = back_value[loader_slot].reshape(tok_rows, row_width)
    return (attn_out, grad_queries, grad_keys, grad_values)


def dot_nn(left, right):
    return lax.dot_general(left, right, (((1,), (0,)), ((), ())), preferred_element_type=F32)


def dot_nt(left, right):
    return lax.dot_general(left, right, (((1,), (1,)), ((), ())), preferred_element_type=F32)


def dot_tn(left, right):
    return lax.dot_general(left, right, (((0,), (0,)), ((), ())), preferred_element_type=F32)


def iota(shape, axis):
    return lax.broadcasted_iota(jnp.int32, shape, axis)


def fused_kernel(
    n_dp,
    n_sp,
    block_rows,
    heads_dev,
    length_ref,
    plan_ref,
    bin_ref,
    table_ref,
    source_ref,
    q_ref,
    k_ref,
    v_ref,
    cot_ref,
    out_ref,
    gq_ref,
    gk_ref,
    gv_ref,
    send_buf,
    recv_buf,
    cot_buf,
    grad_buf,
    back_buf,
    out_buf,
    oback_buf,
    order_buf,
    unorder_buf,
    pick_buf,
    send_sem,
    recv_sem,
    gsend_sem,
    back_sem,
    csend_sem,
    crecv_sem,
    osend_sem,
    orecv_sem,
    local_sem,
):
    n = n_dp * n_sp
    chunk = n_sp * block_rows
    tok = q_ref.shape[0]
    group_tok = tok * n_sp
    group_blocks = group_tok // block_rows
    others = (n - 1) * chunk
    group = lax.axis_index("dp")
    part = lax.axis_index("sp")
    me = group * n_sp + part
    my_rows = pl.ds(pl.multiple_of(me * chunk, chunk), chunk)
    my_group_rows = pl.ds(pl.multiple_of(group * chunk, chunk), chunk)
    my_part_rows = pl.ds(pl.multiple_of(part * tok, tok), tok)

    barrier = pltpu.get_barrier_semaphore()

    def greet(i, carry):
        peer = (me + 1 + i) % n
        pl.semaphore_signal(
            barrier, inc=1, device_id=(peer // n_sp, peer % n_sp), device_id_type=MESH
        )
        return carry

    lax.fori_loop(0, n - 1, greet, 0)

    source = source_ref[...]
    loader_of = source // n
    mine = jnp.where(loader_of == me, source % n, 0)
    spread = jnp.broadcast_to(mine[:, None, :], (n_dp, chunk, group_blocks)).reshape(
        n_dp * chunk, group_blocks
    )
    row_part = (iota((n_dp * chunk, group_blocks), 0) // block_rows) % n_sp
    col_part = iota((n_dp * chunk, group_blocks), 1) // n
    slot = jnp.sum(jnp.where(row_part == col_part, spread, 0), axis=1, keepdims=True)
    pick_row = slot * block_rows + iota((n_dp * chunk, 1), 0) % block_rows
    pick_buf[...] = jnp.where(iota((n_dp * chunk, tok), 1) == pick_row, 1.0, 0.0).astype(BF16)

    def prepare(j):
        for part_to in range(n_sp):
            head = part_to * heads_dev + j
            columns = pl.ds(pl.multiple_of(head * HD, HD), HD)
            for which, ref in enumerate((q_ref, k_ref, v_ref)):
                send_buf[head, which] = dot_nn(pick_buf[...], ref[:, columns]).astype(BF16)

    def peer_at(i):
        turn = n // 2 + i
        peer = (me + turn % n + turn // n) % n
        return peer // n_sp, peer % n_sp

    def forward(j):
        def one(i, carry):
            to_group, to_part = peer_at(i)
            pltpu.make_async_remote_copy(
                src_ref=send_buf.at[
                    to_part * heads_dev + j,
                    :,
                    pl.ds(pl.multiple_of(to_group * chunk, chunk), chunk),
                    :,
                ],
                dst_ref=recv_buf.at[j, :, my_rows, :],
                send_sem=send_sem.at[j],
                recv_sem=recv_sem.at[j],
                device_id=(to_group, to_part),
                device_id_type=MESH,
            ).start()
            return carry

        lax.fori_loop(0, n - 1, one, 0)
        pltpu.make_async_copy(
            send_buf.at[part * heads_dev + j, :, my_group_rows, :],
            recv_buf.at[j, :, my_rows, :],
            local_sem.at[j],
        ).start()

    def backward(j):
        def one(i, carry):
            to_group, to_part = peer_at(i)
            to = to_group * n_sp + to_part
            pltpu.make_async_remote_copy(
                src_ref=grad_buf.at[j, :, pl.ds(pl.multiple_of(to * chunk, chunk), chunk), :],
                dst_ref=back_buf.at[part * heads_dev + j, :, my_group_rows, :],
                send_sem=gsend_sem.at[j],
                recv_sem=back_sem.at[j],
                device_id=(to_group, to_part),
                device_id_type=MESH,
            ).start()
            return carry

        lax.fori_loop(0, n - 1, one, 0)
        pltpu.make_async_copy(
            grad_buf.at[j, :, my_rows, :],
            back_buf.at[part * heads_dev + j, :, my_group_rows, :],
            local_sem.at[heads_dev + j],
        ).start()

        for step in range(1, n_sp):
            to_part = (part + step) % n_sp
            pltpu.make_async_remote_copy(
                src_ref=out_buf.at[j, pl.ds(pl.multiple_of(to_part * tok, tok), tok), :],
                dst_ref=oback_buf.at[part * heads_dev + j],
                send_sem=osend_sem.at[j],
                recv_sem=orecv_sem.at[j],
                device_id=(group, to_part),
                device_id_type=MESH,
            ).start()
        pltpu.make_async_copy(
            out_buf.at[j, my_part_rows, :],
            oback_buf.at[part * heads_dev + j],
            local_sem.at[2 * heads_dev + j],
        ).start()

    def wait_bytes(ref, sem):
        pltpu.make_async_copy(ref, ref, sem).wait()

    width = heads_dev * HD
    prepare(0)
    pl.semaphore_wait(barrier, n - 1)
    forward(0)
    for step in range(1, n_sp):
        to_part = (part + step) % n_sp
        pltpu.make_async_remote_copy(
            src_ref=cot_ref.at[:, pl.ds(pl.multiple_of(to_part * width, HD), width)],
            dst_ref=cot_buf.at[my_part_rows, :],
            send_sem=csend_sem,
            recv_sem=crecv_sem,
            device_id=(group, to_part),
            device_id_type=MESH,
        ).start()
    pltpu.make_async_copy(
        cot_ref.at[:, pl.ds(pl.multiple_of(part * width, HD), width)],
        cot_buf.at[my_part_rows, :],
        local_sem.at[3 * heads_dev],
    ).start()

    def send_more(j, carry):
        prepare(j)
        forward(j)
        return carry

    lax.fori_loop(1, heads_dev, send_more, 0)

    group_len = jnp.int32(0)
    group_bin = jnp.int32(0)
    for sample in range(n_dp):
        picked = plan_ref[sample] == group
        group_len += jnp.where(picked, length_ref[sample], 0)
        group_bin += jnp.where(picked, bin_ref[sample], 0)

    loader_row = (source_ref[pl.ds(group, 1), :] // n).astype(F32)
    widen = jnp.where(
        iota((group_blocks, group_tok), 0) == iota((group_blocks, group_tok), 1) // block_rows,
        1.0,
        0.0,
    ).astype(BF16)
    place = iota((1, group_tok), 1)
    lane_loader = dot_nn(
        jnp.broadcast_to(loader_row, (16, group_blocks)).astype(BF16), widen
    )[0:1].astype(jnp.int32)
    lane_row = lane_loader * chunk + (place // tok) * block_rows + place % block_rows
    col_loader = jnp.sum(
        jnp.where(
            iota((group_tok, group_blocks), 1) == iota((group_tok, group_blocks), 0) // block_rows,
            loader_row,
            0.0,
        ),
        axis=1,
        keepdims=True,
    ).astype(jnp.int32)
    col_place = iota((group_tok, 1), 0)
    col_row = col_loader * chunk + (col_place // tok) * block_rows + col_place % block_rows
    square = (group_tok, group_tok)
    order = jnp.where(iota(square, 0) == lane_row, 1.0, 0.0)
    unorder = jnp.where(iota(square, 1) == col_row, 1.0, 0.0)
    order_buf[...] = order.astype(BF16)
    unorder_buf[...] = unorder.astype(BF16)
    key_live = jnp.sum(jnp.where(place < group_len, order, 0.0), axis=1, keepdims=True)
    query_live = jnp.sum(jnp.where(col_place < group_len, unorder, 0.0), axis=0, keepdims=True)

    wait_bytes(cot_buf.at[pl.ds(0, (n_sp - 1) * tok), :], crecv_sem)
    wait_bytes(cot_buf.at[my_part_rows, :], local_sem.at[3 * heads_dev])

    scale = HD ** (-0.5)

    def one_head(j, carry):
        gate = table_ref[group_bin, part * heads_dev + j]
        columns = pl.ds(pl.multiple_of(j * HD, HD), HD)
        d_out = (gate * dot_nn(order_buf[...], cot_buf[:, columns])).astype(BF16)
        wait_bytes(recv_buf.at[j, :, pl.ds(0, others), :], recv_sem.at[j])
        wait_bytes(recv_buf.at[j, :, my_rows, :], local_sem.at[j])
        query, key, value = recv_buf[j, 0], recv_buf[j, 1], recv_buf[j, 2]
        scores = dot_nt(key, query) * scale
        scores = jnp.where(key_live > 0.5, scores, -1e30)
        top = jnp.max(scores, axis=0, keepdims=True)
        shifted = jnp.exp(scores - top)
        total = jnp.sum(shifted, axis=0, keepdims=True)
        attend = shifted * (query_live / total)
        attend_bf = attend.astype(BF16)
        grad_attend = dot_nt(value, d_out)
        row_dot = jnp.sum(attend_bf.astype(F32) * grad_attend, axis=0, keepdims=True)
        grad_scores = (attend * (grad_attend - row_dot) * scale).astype(BF16)
        grad_buf[j, 2] = dot_nn(attend_bf, d_out).astype(BF16)
        grad_buf[j, 1] = dot_nn(grad_scores, query).astype(BF16)
        grad_buf[j, 0] = dot_tn(grad_scores, key).astype(BF16)
        output = dot_tn(attend_bf, value).astype(BF16)
        gated = (gate * output.astype(F32)).astype(BF16)
        out_buf[j] = dot_nn(unorder_buf[...], gated).astype(BF16)
        backward(j)
        return carry

    lax.fori_loop(0, heads_dev, one_head, 0)

    def collect(j, carry):
        wait_bytes(recv_buf.at[j, :, pl.ds(0, others), :], back_sem.at[j])
        wait_bytes(recv_buf.at[j, :, my_rows, :], local_sem.at[heads_dev + j])
        wait_bytes(out_buf.at[j, pl.ds(0, (n_sp - 1) * tok), :], orecv_sem.at[j])
        wait_bytes(out_buf.at[j, my_part_rows, :], local_sem.at[2 * heads_dev + j])
        for part_from in range(n_sp):
            head = part_from * heads_dev + j
            columns = pl.ds(pl.multiple_of(head * HD, HD), HD)
            out_ref[:, columns] = oback_buf[head]
            for which, ref in enumerate((gq_ref, gk_ref, gv_ref)):
                ref[:, columns] = dot_tn(pick_buf[...], back_buf[head, which]).astype(BF16)
        return carry

    lax.fori_loop(0, heads_dev, collect, 0)

    def drain(j, carry):
        wait_bytes(recv_buf.at[j, :, pl.ds(0, others), :], send_sem.at[j])
        wait_bytes(recv_buf.at[j, :, pl.ds(0, others), :], gsend_sem.at[j])
        wait_bytes(out_buf.at[j, pl.ds(0, (n_sp - 1) * tok), :], osend_sem.at[j])
        return carry

    lax.fori_loop(0, heads_dev, drain, 0)
    wait_bytes(cot_buf.at[pl.ds(0, (n_sp - 1) * tok), :], csend_sem)


def fused(
    n_dp,
    n_sp,
    queries,
    key_rows,
    value_rows,
    cotangent,
    lengths,
    sample_plan,
    guide_bins,
    guide_table,
    block_source,
):
    tok, row_width = queries.shape
    n = n_dp * n_sp
    heads_dev = HEADS // n_sp
    group_tok = tok * n_sp
    smem = pl.BlockSpec(memory_space=pltpu.SMEM)
    vmem = pl.BlockSpec(memory_space=pltpu.VMEM)
    flops = 2 * 8 * heads_dev * group_tok * group_tok * HD
    return pl.pallas_call(
        functools.partial(fused_kernel, n_dp, n_sp, tok // n, heads_dev),
        out_shape=[jax.ShapeDtypeStruct((tok, row_width), BF16)] * 4,
        in_specs=[smem] * 4 + [vmem] * 5,
        out_specs=[vmem] * 4,
        scratch_shapes=[
            pltpu.VMEM((HEADS, 3, tok, HD), BF16),
            pltpu.VMEM((heads_dev, 3, group_tok, HD), BF16),
            pltpu.VMEM((group_tok, heads_dev * HD), BF16),
            pltpu.VMEM((heads_dev, 3, group_tok, HD), BF16),
            pltpu.VMEM((HEADS, 3, tok, HD), BF16),
            pltpu.VMEM((heads_dev, group_tok, HD), BF16),
            pltpu.VMEM((HEADS, tok, HD), BF16),
            pltpu.VMEM((group_tok, group_tok), BF16),
            pltpu.VMEM((group_tok, group_tok), BF16),
            pltpu.VMEM((tok, tok), BF16),
            pltpu.SemaphoreType.DMA((heads_dev,)),
            pltpu.SemaphoreType.DMA((heads_dev,)),
            pltpu.SemaphoreType.DMA((heads_dev,)),
            pltpu.SemaphoreType.DMA((heads_dev,)),
            pltpu.SemaphoreType.DMA,
            pltpu.SemaphoreType.DMA,
            pltpu.SemaphoreType.DMA((heads_dev,)),
            pltpu.SemaphoreType.DMA((heads_dev,)),
            pltpu.SemaphoreType.DMA((3 * heads_dev + 1,)),
        ],
        compiler_params=pltpu.CompilerParams(
            collective_id=0, has_side_effects=True, vmem_limit_bytes=48 * 1024 * 1024
        ),
        cost_estimate=pl.CostEstimate(
            flops=flops, bytes_accessed=16 * tok * row_width, transcendentals=0
        ),
        name="routed_attention",
    )(
        lengths,
        sample_plan,
        guide_bins,
        guide_table,
        block_source.reshape(n_dp, block_source.shape[0] // n_dp),
        queries,
        key_rows,
        value_rows,
        cotangent,
    )


def chosen(*arrays):
    n_dp, n_sp = lax.axis_size("dp"), lax.axis_size("sp")
    tok = arrays[0].shape[0]
    block_rows = tok // (n_dp * n_sp)
    if (n_sp * block_rows) % 16 == 0 and HEADS % n_sp == 0:
        return fused(n_dp, n_sp, *arrays)
    return per_device(*arrays)


def solution(mesh):
    placed = (
        P(("dp", "sp"), None),
        P(("dp", "sp"), None),
        P(("dp", "sp"), None),
        P(("dp", "sp"), None),
        P(),
        P(),
        P(),
        P(),
        P(),
    )
    return jax.shard_map(
        chosen,
        mesh=mesh,
        in_specs=placed,
        out_specs=(
            P(("dp", "sp"), None),
            P(("dp", "sp"), None),
            P(("dp", "sp"), None),
            P(("dp", "sp"), None),
        ),
        check_vma=False,
    )
```

```python
import functools

import jax
import jax.numpy as jnp
from jax import lax
from jax.experimental import pallas as pl
from jax.experimental.pallas import tpu as pltpu
from jax.sharding import PartitionSpec as P

HEADS = 20
HD = 128
MESH = pl.DeviceIdType.MESH
VMEM_GRANT = 62 * 1024 * 1024
F32 = jnp.float32
BF16 = jnp.bfloat16


def head_pass(query_head, key_head, value_head, grad_head, query_live, key_live):
    scores = jnp.dot(query_head, key_head.T, preferred_element_type=jnp.float32) * HD ** (-0.5)
    masked = jnp.where(key_live[None, :], scores, -1e30)
    top_score = jnp.max(masked, axis=1, keepdims=True)
    shifted_exp = jnp.where(key_live[None, :], jnp.exp(masked - top_score), 0.0)
    row_total = jnp.sum(shifted_exp, axis=1, keepdims=True)
    attend = jnp.where(query_live[:, None], shifted_exp / row_total, 0.0)
    attend_bf = attend.astype(jnp.bfloat16)
    output = jnp.dot(attend_bf, value_head, preferred_element_type=jnp.float32)
    grad_attend = jnp.dot(grad_head, value_head.T, preferred_element_type=jnp.float32)
    row_dot = jnp.sum(grad_head.astype(jnp.float32) * output, axis=1, keepdims=True)
    grad_scores = (attend * (grad_attend - row_dot) * HD ** (-0.5)).astype(jnp.bfloat16)
    grad_query = jnp.dot(grad_scores, key_head, preferred_element_type=jnp.float32)
    grad_key = jnp.dot(grad_scores.T, query_head, preferred_element_type=jnp.float32)
    grad_value = jnp.dot(attend_bf.T, grad_head, preferred_element_type=jnp.float32)
    return (output, grad_query, grad_key, grad_value)


def head_stack(query_part, key_part, value_part, grad_part, query_live, key_live):

    def one_head(head_items):
        return head_pass(
            head_items[0], head_items[1], head_items[2], head_items[3], query_live, key_live
        )

    stacked = tuple(
        (jnp.moveaxis(source, 1, 0) for source in (query_part, key_part, value_part, grad_part))
    )
    return lax.map(one_head, stacked)


def dispatch(first, second, third):
    return (
        lax.all_to_all(first, ("dp", "sp"), split_axis=0, concat_axis=0, tiled=True),
        lax.all_to_all(second, ("dp", "sp"), split_axis=0, concat_axis=0, tiled=True),
        lax.all_to_all(third, ("dp", "sp"), split_axis=0, concat_axis=0, tiled=True),
    )


def send_back(first, second, third):
    return (
        lax.all_to_all(first, ("dp", "sp"), split_axis=0, concat_axis=0, tiled=True),
        lax.all_to_all(second, ("dp", "sp"), split_axis=0, concat_axis=0, tiled=True),
        lax.all_to_all(third, ("dp", "sp"), split_axis=0, concat_axis=0, tiled=True),
    )


def per_device(
    queries,
    key_rows,
    value_rows,
    cotangent,
    lengths,
    sample_plan,
    guide_bins,
    guide_table,
    block_source,
):
    n_dp = lax.axis_size("dp")
    n_sp = lax.axis_size("sp")
    loaders = n_dp * n_sp
    tok_rows = queries.shape[0]
    row_width = queries.shape[1]
    block_rows = tok_rows // loaders
    device_index = lax.axis_index("dp") * n_sp + lax.axis_index("sp")
    table = block_source.reshape(loaders, loaders)
    sources = table[device_index] // loaders
    send_slot = jnp.sum(jnp.where(table // loaders == device_index, table % loaders, 0), axis=1)
    slot_index = jnp.arange(loaders, dtype=jnp.int32)
    back_slot = jnp.sum(
        jnp.where(sources[None, :] == slot_index[:, None], slot_index[None, :], 0), axis=1
    )
    loader_slot = jnp.sum(
        jnp.where(send_slot[None, :] == slot_index[:, None], slot_index[None, :], 0), axis=1
    )

    def as_blocks(source, order):
        return source.reshape(loaders, block_rows, row_width)[order]

    recv_query, recv_key, recv_value = dispatch(
        as_blocks(queries, send_slot),
        as_blocks(key_rows, send_slot),
        as_blocks(value_rows, send_slot),
    )
    query_own = recv_query[sources].reshape(tok_rows, HEADS, HD)
    key_own = recv_key[sources].reshape(tok_rows, HEADS, HD)
    value_own = recv_value[sources].reshape(tok_rows, HEADS, HD)
    group_index = lax.axis_index("dp")
    picked = sample_plan == group_index
    group_len = jnp.sum(jnp.where(picked, lengths, 0))
    group_bin = jnp.sum(jnp.where(picked, guide_bins, 0))
    bin_match = jnp.arange(guide_table.shape[0], dtype=jnp.int32) == group_bin
    head_gate = jnp.sum(jnp.where(bin_match[:, None], guide_table, 0.0), axis=0)
    grad_own = (
        head_gate[None, :, None] * cotangent.reshape(tok_rows, HEADS, HD).astype(jnp.float32)
    ).astype(jnp.bfloat16)
    heads_dev = HEADS // n_sp
    split_shape = (tok_rows, n_sp, heads_dev, HD)
    group_items = (
        lax.all_to_all(
            query_own.reshape(split_shape), "sp", split_axis=1, concat_axis=0, tiled=True
        ),
        lax.all_to_all(key_own.reshape(split_shape), "sp", split_axis=1, concat_axis=0, tiled=True),
        lax.all_to_all(
            value_own.reshape(split_shape), "sp", split_axis=1, concat_axis=0, tiled=True
        ),
        lax.all_to_all(
            grad_own.reshape(split_shape), "sp", split_axis=1, concat_axis=0, tiled=True
        ),
    )
    flat_items = tuple((item[:, 0] for item in group_items))
    live_rows = jnp.arange(flat_items[0].shape[0], dtype=jnp.int32) < group_len
    results = head_stack(
        flat_items[0], flat_items[1], flat_items[2], flat_items[3], live_rows, live_rows
    )
    out_heads, gq_heads, gk_heads, gv_heads = tuple(
        (jnp.moveaxis(result, 0, 1)[:, None].astype(jnp.bfloat16) for result in results)
    )
    back_rows = (
        lax.all_to_all(out_heads, "sp", split_axis=0, concat_axis=1, tiled=True),
        lax.all_to_all(gq_heads, "sp", split_axis=0, concat_axis=1, tiled=True),
        lax.all_to_all(gk_heads, "sp", split_axis=0, concat_axis=1, tiled=True),
        lax.all_to_all(gv_heads, "sp", split_axis=0, concat_axis=1, tiled=True),
    )
    out_bf, grad_q_own, grad_k_own, grad_v_own = tuple(
        (part.reshape(tok_rows, HEADS, HD) for part in back_rows)
    )
    attn_out = (
        (head_gate[None, :, None] * lax.optimization_barrier(out_bf).astype(jnp.float32))
        .astype(jnp.bfloat16)
        .reshape(tok_rows, row_width)
    )
    back_query, back_key, back_value = send_back(
        as_blocks(grad_q_own, back_slot),
        as_blocks(grad_k_own, back_slot),
        as_blocks(grad_v_own, back_slot),
    )
    grad_queries = back_query[loader_slot].reshape(tok_rows, row_width)
    grad_keys = back_key[loader_slot].reshape(tok_rows, row_width)
    grad_values = back_value[loader_slot].reshape(tok_rows, row_width)
    return (attn_out, grad_queries, grad_keys, grad_values)


def dot_nn(left, right):
    return lax.dot_general(left, right, (((1,), (0,)), ((), ())), preferred_element_type=F32)


def dot_nt(left, right):
    return lax.dot_general(left, right, (((1,), (1,)), ((), ())), preferred_element_type=F32)


def dot_tn(left, right):
    return lax.dot_general(left, right, (((0,), (0,)), ((), ())), preferred_element_type=F32)


def iota(shape, axis):
    return lax.broadcasted_iota(jnp.int32, shape, axis)


def fused_kernel(
    n_dp,
    n_sp,
    block_rows,
    heads_dev,
    length_ref,
    plan_ref,
    bin_ref,
    table_ref,
    source_ref,
    q_ref,
    k_ref,
    v_ref,
    cot_ref,
    out_ref,
    gq_ref,
    gk_ref,
    gv_ref,
    load_buf,
    send_buf,
    recv_buf,
    cot_buf,
    grad_buf,
    back_buf,
    out_buf,
    oback_buf,
    order_buf,
    unorder_buf,
    pick_buf,
    stage_buf,
    load_sem,
    send_sem,
    recv_sem,
    gsend_sem,
    back_sem,
    csend_sem,
    crecv_sem,
    osend_sem,
    orecv_sem,
    local_sem,
    store_sem,
):
    n = n_dp * n_sp
    chunk = n_sp * block_rows
    tok = q_ref.shape[0]
    group_tok = tok * n_sp
    group_blocks = group_tok // block_rows
    others = (n - 1) * chunk
    group = lax.axis_index("dp")
    part = lax.axis_index("sp")
    me = group * n_sp + part
    my_rows = pl.ds(pl.multiple_of(me * chunk, chunk), chunk)
    my_group_rows = pl.ds(pl.multiple_of(group * chunk, chunk), chunk)
    my_part_rows = pl.ds(pl.multiple_of(part * tok, tok), tok)

    def load(j, carry):
        for part_to in range(n_sp):
            columns = pl.ds(pl.multiple_of((part_to * heads_dev + j) * HD, HD), HD)
            for which, ref in enumerate((q_ref, k_ref, v_ref)):
                pltpu.make_async_copy(
                    ref.at[:, columns], load_buf.at[j, part_to, which], load_sem.at[j]
                ).start()
        return carry

    barrier = pltpu.get_barrier_semaphore()
    load(0, 0)

    def greet(i, carry):
        peer = (me + 1 + i) % n
        pl.semaphore_signal(
            barrier, inc=1, device_id=(peer // n_sp, peer % n_sp), device_id_type=MESH
        )
        return carry

    lax.fori_loop(0, n - 1, greet, 0)
    lax.fori_loop(1, heads_dev, load, 0)

    source = source_ref[...]
    loader_of = source // n
    mine = jnp.where(loader_of == me, source % n, 0)
    spread = jnp.broadcast_to(mine[:, None, :], (n_dp, chunk, group_blocks)).reshape(
        n_dp * chunk, group_blocks
    )
    row_part = (iota((n_dp * chunk, group_blocks), 0) // block_rows) % n_sp
    col_part = iota((n_dp * chunk, group_blocks), 1) // n
    slot = jnp.sum(jnp.where(row_part == col_part, spread, 0), axis=1, keepdims=True)
    pick_row = slot * block_rows + iota((n_dp * chunk, 1), 0) % block_rows
    pick_buf[...] = jnp.where(iota((n_dp * chunk, tok), 1) == pick_row, 1.0, 0.0).astype(BF16)

    def wait_bytes(ref, sem):
        pltpu.make_async_copy(ref, ref, sem).wait()

    def prepare(j):
        wait_bytes(load_buf.at[j], load_sem.at[j])
        for part_to in range(n_sp):
            head = part_to * heads_dev + j
            for which in range(3):
                send_buf[head, which] = dot_nn(
                    pick_buf[...], load_buf[j, part_to, which]
                ).astype(BF16)

    def peer_at(i):
        turn = i + (i + n - 3) // (n - 1)
        quarter = n // 4
        outer = (me // quarter + 6 - turn % 4) % 4
        peer = outer * quarter + (me % quarter + turn // 4) % quarter
        return peer // n_sp, peer % n_sp

    def forward(j):
        def one(i, carry):
            to_group, to_part = peer_at(i)
            pltpu.make_async_remote_copy(
                src_ref=send_buf.at[
                    to_part * heads_dev + j,
                    :,
                    pl.ds(pl.multiple_of(to_group * chunk, chunk), chunk),
                    :,
                ],
                dst_ref=recv_buf.at[j, :, my_rows, :],
                send_sem=send_sem.at[j],
                recv_sem=recv_sem.at[j],
                device_id=(to_group, to_part),
                device_id_type=MESH,
            ).start()
            return carry

        lax.fori_loop(0, n - 1, one, 0)
        pltpu.make_async_copy(
            send_buf.at[part * heads_dev + j, :, my_group_rows, :],
            recv_buf.at[j, :, my_rows, :],
            local_sem.at[j],
        ).start()

    def backward(j):
        def one(i, carry):
            to_group, to_part = peer_at(i)
            to = to_group * n_sp + to_part
            pltpu.make_async_remote_copy(
                src_ref=grad_buf.at[j, :, pl.ds(pl.multiple_of(to * chunk, chunk), chunk), :],
                dst_ref=back_buf.at[part * heads_dev + j, :, my_group_rows, :],
                send_sem=gsend_sem.at[j],
                recv_sem=back_sem.at[j],
                device_id=(to_group, to_part),
                device_id_type=MESH,
            ).start()
            return carry

        lax.fori_loop(0, n - 1, one, 0)
        pltpu.make_async_copy(
            grad_buf.at[j, :, my_rows, :],
            back_buf.at[part * heads_dev + j, :, my_group_rows, :],
            local_sem.at[heads_dev + j],
        ).start()

        for step in range(1, n_sp):
            to_part = (part + step) % n_sp
            pltpu.make_async_remote_copy(
                src_ref=out_buf.at[j, pl.ds(pl.multiple_of(to_part * tok, tok), tok), :],
                dst_ref=oback_buf.at[part * heads_dev + j],
                send_sem=osend_sem.at[j],
                recv_sem=orecv_sem.at[j],
                device_id=(group, to_part),
                device_id_type=MESH,
            ).start()
        pltpu.make_async_copy(
            out_buf.at[j, my_part_rows, :],
            oback_buf.at[part * heads_dev + j],
            local_sem.at[2 * heads_dev + j],
        ).start()

    width = heads_dev * HD
    prepare(0)
    pl.semaphore_wait(barrier, n - 1)
    forward(0)
    for step in range(1, n_sp):
        to_part = (part + step) % n_sp
        pltpu.make_async_remote_copy(
            src_ref=cot_ref.at[:, pl.ds(pl.multiple_of(to_part * width, HD), width)],
            dst_ref=cot_buf.at[my_part_rows, :],
            send_sem=csend_sem,
            recv_sem=crecv_sem,
            device_id=(group, to_part),
            device_id_type=MESH,
        ).start()
    pltpu.make_async_copy(
        cot_ref.at[:, pl.ds(pl.multiple_of(part * width, HD), width)],
        cot_buf.at[my_part_rows, :],
        local_sem.at[3 * heads_dev],
    ).start()

    def send_more(j, carry):
        prepare(j)
        forward(j)
        return carry

    lax.fori_loop(1, heads_dev, send_more, 0)

    group_len = jnp.int32(0)
    group_bin = jnp.int32(0)
    for sample in range(n_dp):
        picked = plan_ref[sample] == group
        group_len += jnp.where(picked, length_ref[sample], 0)
        group_bin += jnp.where(picked, bin_ref[sample], 0)

    loader_row = (source_ref[pl.ds(group, 1), :] // n).astype(F32)
    widen = jnp.where(
        iota((group_blocks, group_tok), 0) == iota((group_blocks, group_tok), 1) // block_rows,
        1.0,
        0.0,
    ).astype(BF16)
    place = iota((1, group_tok), 1)
    lane_loader = dot_nn(
        jnp.broadcast_to(loader_row, (16, group_blocks)).astype(BF16), widen
    )[0:1].astype(jnp.int32)
    lane_row = lane_loader * chunk + (place // tok) * block_rows + place % block_rows
    col_loader = jnp.sum(
        jnp.where(
            iota((group_tok, group_blocks), 1) == iota((group_tok, group_blocks), 0) // block_rows,
            loader_row,
            0.0,
        ),
        axis=1,
        keepdims=True,
    ).astype(jnp.int32)
    col_place = iota((group_tok, 1), 0)
    col_row = col_loader * chunk + (col_place // tok) * block_rows + col_place % block_rows
    square = (group_tok, group_tok)
    order = jnp.where(iota(square, 0) == lane_row, 1.0, 0.0)
    unorder = jnp.where(iota(square, 1) == col_row, 1.0, 0.0)
    order_buf[...] = order.astype(BF16)
    unorder_buf[...] = unorder.astype(BF16)
    key_live = jnp.sum(jnp.where(place < group_len, order, 0.0), axis=1, keepdims=True)
    query_live = jnp.sum(jnp.where(col_place < group_len, unorder, 0.0), axis=0, keepdims=True)

    wait_bytes(cot_buf.at[pl.ds(0, (n_sp - 1) * tok), :], crecv_sem)
    wait_bytes(cot_buf.at[my_part_rows, :], local_sem.at[3 * heads_dev])

    scale = HD ** (-0.5)

    def one_head(j, carry):
        gate = table_ref[group_bin, part * heads_dev + j]
        columns = pl.ds(pl.multiple_of(j * HD, HD), HD)
        d_out = (gate * dot_nn(order_buf[...], cot_buf[:, columns])).astype(BF16)
        wait_bytes(recv_buf.at[j, :, pl.ds(0, others), :], recv_sem.at[j])
        wait_bytes(recv_buf.at[j, :, my_rows, :], local_sem.at[j])
        query, key, value = recv_buf[j, 0], recv_buf[j, 1], recv_buf[j, 2]
        scores = dot_nt(key, query) * scale
        scores = jnp.where(key_live > 0.5, scores, -1e30)
        top = jnp.max(scores, axis=0, keepdims=True)
        shifted = jnp.exp(scores - top)
        total = jnp.sum(shifted, axis=0, keepdims=True)
        attend = shifted * (query_live / total)
        attend_bf = attend.astype(BF16)
        grad_attend = dot_nt(value, d_out)
        row_dot = jnp.sum(attend_bf.astype(F32) * grad_attend, axis=0, keepdims=True)
        grad_scores = (attend * (grad_attend - row_dot) * scale).astype(BF16)
        grad_buf[j, 2] = dot_nn(attend_bf, d_out).astype(BF16)
        grad_buf[j, 1] = dot_nn(grad_scores, query).astype(BF16)
        grad_buf[j, 0] = dot_tn(grad_scores, key).astype(BF16)
        output = dot_tn(attend_bf, value).astype(BF16)
        gated = (gate * output.astype(F32)).astype(BF16)
        out_buf[j] = dot_nn(unorder_buf[...], gated).astype(BF16)
        backward(j)
        return carry

    lax.fori_loop(0, heads_dev, one_head, 0)

    def collect(j, carry):
        wait_bytes(recv_buf.at[j, :, pl.ds(0, others), :], back_sem.at[j])
        wait_bytes(recv_buf.at[j, :, my_rows, :], local_sem.at[heads_dev + j])
        wait_bytes(out_buf.at[j, pl.ds(0, (n_sp - 1) * tok), :], orecv_sem.at[j])
        wait_bytes(out_buf.at[j, my_part_rows, :], local_sem.at[2 * heads_dev + j])
        for part_from in range(n_sp):
            head = part_from * heads_dev + j
            columns = pl.ds(pl.multiple_of(head * HD, HD), HD)
            pltpu.make_async_copy(
                oback_buf.at[head], out_ref.at[:, columns], store_sem.at[0]
            ).start()
            for which, ref in enumerate((gq_ref, gk_ref, gv_ref)):
                stage_buf[head, which] = dot_tn(pick_buf[...], back_buf[head, which]).astype(BF16)
                pltpu.make_async_copy(
                    stage_buf.at[head, which], ref.at[:, columns], store_sem.at[1 + which]
                ).start()
        return carry

    lax.fori_loop(0, heads_dev, collect, 0)

    def drain(j, carry):
        wait_bytes(recv_buf.at[j, :, pl.ds(0, others), :], send_sem.at[j])
        wait_bytes(recv_buf.at[j, :, pl.ds(0, others), :], gsend_sem.at[j])
        wait_bytes(out_buf.at[j, pl.ds(0, (n_sp - 1) * tok), :], osend_sem.at[j])
        return carry

    lax.fori_loop(0, heads_dev, drain, 0)
    wait_bytes(cot_buf.at[pl.ds(0, (n_sp - 1) * tok), :], csend_sem)
    for which in range(4):
        wait_bytes(oback_buf, store_sem.at[which])


def place_kernel(*refs):
    sources, targets, sems = refs[:4], refs[4:8], refs[8]
    rows = 32
    copies = []
    for which in range(4):
        for piece in range(sources[which].shape[0] // rows):
            part = pl.ds(piece * rows, rows)
            copies.append(
                pltpu.make_async_copy(
                    sources[which].at[part, :], targets[which].at[part, :], sems.at[len(copies)]
                )
            )
            copies[-1].start()
    for copy in copies:
        copy.wait()


def place_outputs(results):
    hbm = pl.BlockSpec(memory_space=pltpu.HBM)
    pieces = sum(result.shape[0] // 32 for result in results)
    return pl.pallas_call(
        place_kernel,
        out_shape=[jax.ShapeDtypeStruct(result.shape, BF16) for result in results],
        in_specs=[hbm] * 4,
        out_specs=[hbm] * 4,
        scratch_shapes=[pltpu.SemaphoreType.DMA((pieces,))],
        compiler_params=pltpu.CompilerParams(vmem_limit_bytes=VMEM_GRANT),
        name="place_outputs",
    )(*results)


def fused(
    n_dp,
    n_sp,
    queries,
    key_rows,
    value_rows,
    cotangent,
    lengths,
    sample_plan,
    guide_bins,
    guide_table,
    block_source,
):
    tok, row_width = queries.shape
    n = n_dp * n_sp
    heads_dev = HEADS // n_sp
    group_tok = tok * n_sp
    smem = pl.BlockSpec(memory_space=pltpu.SMEM)
    vmem = pl.BlockSpec(memory_space=pltpu.VMEM)
    hbm = pl.BlockSpec(memory_space=pltpu.HBM)
    flops = 2 * 8 * heads_dev * group_tok * group_tok * HD
    return pl.pallas_call(
        functools.partial(fused_kernel, n_dp, n_sp, tok // n, heads_dev),
        out_shape=[jax.ShapeDtypeStruct((tok, row_width), BF16)] * 4,
        in_specs=[smem] * 4 + [vmem] + [hbm] * 4,
        out_specs=[hbm] * 4,
        scratch_shapes=[
            pltpu.VMEM((heads_dev, n_sp, 3, tok, HD), BF16),
            pltpu.VMEM((HEADS, 3, tok, HD), BF16),
            pltpu.VMEM((heads_dev, 3, group_tok, HD), BF16),
            pltpu.VMEM((group_tok, heads_dev * HD), BF16),
            pltpu.VMEM((heads_dev, 3, group_tok, HD), BF16),
            pltpu.VMEM((HEADS, 3, tok, HD), BF16),
            pltpu.VMEM((heads_dev, group_tok, HD), BF16),
            pltpu.VMEM((HEADS, tok, HD), BF16),
            pltpu.VMEM((group_tok, group_tok), BF16),
            pltpu.VMEM((group_tok, group_tok), BF16),
            pltpu.VMEM((tok, tok), BF16),
            pltpu.VMEM((HEADS, 3, tok, HD), BF16),
            pltpu.SemaphoreType.DMA((heads_dev,)),
            pltpu.SemaphoreType.DMA((heads_dev,)),
            pltpu.SemaphoreType.DMA((heads_dev,)),
            pltpu.SemaphoreType.DMA((heads_dev,)),
            pltpu.SemaphoreType.DMA((heads_dev,)),
            pltpu.SemaphoreType.DMA,
            pltpu.SemaphoreType.DMA,
            pltpu.SemaphoreType.DMA((heads_dev,)),
            pltpu.SemaphoreType.DMA((heads_dev,)),
            pltpu.SemaphoreType.DMA((3 * heads_dev + 1,)),
            pltpu.SemaphoreType.DMA((4,)),
        ],
        compiler_params=pltpu.CompilerParams(
            collective_id=0, has_side_effects=True, vmem_limit_bytes=VMEM_GRANT
        ),
        cost_estimate=pl.CostEstimate(
            flops=flops, bytes_accessed=16 * tok * row_width, transcendentals=0
        ),
        name="routed_attention",
    )(
        lengths,
        sample_plan,
        guide_bins,
        guide_table,
        block_source.reshape(n_dp, block_source.shape[0] // n_dp),
        queries,
        key_rows,
        value_rows,
        cotangent,
    )


def chosen(*arrays):
    n_dp, n_sp = lax.axis_size("dp"), lax.axis_size("sp")
    tok = arrays[0].shape[0]
    block_rows = tok // (n_dp * n_sp)
    if (n_sp * block_rows) % 16 == 0 and HEADS % n_sp == 0:
        return place_outputs(fused(n_dp, n_sp, *arrays))
    return per_device(*arrays)


def solution(mesh):
    placed = (
        P(("dp", "sp"), None),
        P(("dp", "sp"), None),
        P(("dp", "sp"), None),
        P(("dp", "sp"), None),
        P(),
        P(),
        P(),
        P(),
        P(),
    )
    return jax.shard_map(
        chosen,
        mesh=mesh,
        in_specs=placed,
        out_specs=(
            P(("dp", "sp"), None),
            P(("dp", "sp"), None),
            P(("dp", "sp"), None),
            P(("dp", "sp"), None),
        ),
        check_vma=False,
    )
```

```python
import functools

import jax
import jax.numpy as jnp
from jax import lax
from jax.experimental import pallas as pl
from jax.experimental.pallas import tpu as pltpu
from jax.sharding import PartitionSpec as P

HEADS = 20
HD = 128
MESH = pl.DeviceIdType.MESH
VMEM_GRANT = 62 * 1024 * 1024
F32 = jnp.float32
BF16 = jnp.bfloat16


def head_pass(query_head, key_head, value_head, grad_head, query_live, key_live):
    scores = jnp.dot(query_head, key_head.T, preferred_element_type=jnp.float32) * HD ** (-0.5)
    masked = jnp.where(key_live[None, :], scores, -1e30)
    top_score = jnp.max(masked, axis=1, keepdims=True)
    shifted_exp = jnp.where(key_live[None, :], jnp.exp(masked - top_score), 0.0)
    row_total = jnp.sum(shifted_exp, axis=1, keepdims=True)
    attend = jnp.where(query_live[:, None], shifted_exp / row_total, 0.0)
    attend_bf = attend.astype(jnp.bfloat16)
    output = jnp.dot(attend_bf, value_head, preferred_element_type=jnp.float32)
    grad_attend = jnp.dot(grad_head, value_head.T, preferred_element_type=jnp.float32)
    row_dot = jnp.sum(grad_head.astype(jnp.float32) * output, axis=1, keepdims=True)
    grad_scores = (attend * (grad_attend - row_dot) * HD ** (-0.5)).astype(jnp.bfloat16)
    grad_query = jnp.dot(grad_scores, key_head, preferred_element_type=jnp.float32)
    grad_key = jnp.dot(grad_scores.T, query_head, preferred_element_type=jnp.float32)
    grad_value = jnp.dot(attend_bf.T, grad_head, preferred_element_type=jnp.float32)
    return (output, grad_query, grad_key, grad_value)


def head_stack(query_part, key_part, value_part, grad_part, query_live, key_live):

    def one_head(head_items):
        return head_pass(
            head_items[0], head_items[1], head_items[2], head_items[3], query_live, key_live
        )

    stacked = tuple(
        (jnp.moveaxis(source, 1, 0) for source in (query_part, key_part, value_part, grad_part))
    )
    return lax.map(one_head, stacked)


def dispatch(first, second, third):
    return (
        lax.all_to_all(first, ("dp", "sp"), split_axis=0, concat_axis=0, tiled=True),
        lax.all_to_all(second, ("dp", "sp"), split_axis=0, concat_axis=0, tiled=True),
        lax.all_to_all(third, ("dp", "sp"), split_axis=0, concat_axis=0, tiled=True),
    )


def send_back(first, second, third):
    return (
        lax.all_to_all(first, ("dp", "sp"), split_axis=0, concat_axis=0, tiled=True),
        lax.all_to_all(second, ("dp", "sp"), split_axis=0, concat_axis=0, tiled=True),
        lax.all_to_all(third, ("dp", "sp"), split_axis=0, concat_axis=0, tiled=True),
    )


def per_device(
    queries,
    key_rows,
    value_rows,
    cotangent,
    lengths,
    sample_plan,
    guide_bins,
    guide_table,
    block_source,
):
    n_dp = lax.axis_size("dp")
    n_sp = lax.axis_size("sp")
    loaders = n_dp * n_sp
    tok_rows = queries.shape[0]
    row_width = queries.shape[1]
    block_rows = tok_rows // loaders
    device_index = lax.axis_index("dp") * n_sp + lax.axis_index("sp")
    table = block_source.reshape(loaders, loaders)
    sources = table[device_index] // loaders
    send_slot = jnp.sum(jnp.where(table // loaders == device_index, table % loaders, 0), axis=1)
    slot_index = jnp.arange(loaders, dtype=jnp.int32)
    back_slot = jnp.sum(
        jnp.where(sources[None, :] == slot_index[:, None], slot_index[None, :], 0), axis=1
    )
    loader_slot = jnp.sum(
        jnp.where(send_slot[None, :] == slot_index[:, None], slot_index[None, :], 0), axis=1
    )

    def as_blocks(source, order):
        return source.reshape(loaders, block_rows, row_width)[order]

    recv_query, recv_key, recv_value = dispatch(
        as_blocks(queries, send_slot),
        as_blocks(key_rows, send_slot),
        as_blocks(value_rows, send_slot),
    )
    query_own = recv_query[sources].reshape(tok_rows, HEADS, HD)
    key_own = recv_key[sources].reshape(tok_rows, HEADS, HD)
    value_own = recv_value[sources].reshape(tok_rows, HEADS, HD)
    group_index = lax.axis_index("dp")
    picked = sample_plan == group_index
    group_len = jnp.sum(jnp.where(picked, lengths, 0))
    group_bin = jnp.sum(jnp.where(picked, guide_bins, 0))
    bin_match = jnp.arange(guide_table.shape[0], dtype=jnp.int32) == group_bin
    head_gate = jnp.sum(jnp.where(bin_match[:, None], guide_table, 0.0), axis=0)
    grad_own = (
        head_gate[None, :, None] * cotangent.reshape(tok_rows, HEADS, HD).astype(jnp.float32)
    ).astype(jnp.bfloat16)
    heads_dev = HEADS // n_sp
    split_shape = (tok_rows, n_sp, heads_dev, HD)
    group_items = (
        lax.all_to_all(
            query_own.reshape(split_shape), "sp", split_axis=1, concat_axis=0, tiled=True
        ),
        lax.all_to_all(key_own.reshape(split_shape), "sp", split_axis=1, concat_axis=0, tiled=True),
        lax.all_to_all(
            value_own.reshape(split_shape), "sp", split_axis=1, concat_axis=0, tiled=True
        ),
        lax.all_to_all(
            grad_own.reshape(split_shape), "sp", split_axis=1, concat_axis=0, tiled=True
        ),
    )
    flat_items = tuple((item[:, 0] for item in group_items))
    live_rows = jnp.arange(flat_items[0].shape[0], dtype=jnp.int32) < group_len
    results = head_stack(
        flat_items[0], flat_items[1], flat_items[2], flat_items[3], live_rows, live_rows
    )
    out_heads, gq_heads, gk_heads, gv_heads = tuple(
        (jnp.moveaxis(result, 0, 1)[:, None].astype(jnp.bfloat16) for result in results)
    )
    back_rows = (
        lax.all_to_all(out_heads, "sp", split_axis=0, concat_axis=1, tiled=True),
        lax.all_to_all(gq_heads, "sp", split_axis=0, concat_axis=1, tiled=True),
        lax.all_to_all(gk_heads, "sp", split_axis=0, concat_axis=1, tiled=True),
        lax.all_to_all(gv_heads, "sp", split_axis=0, concat_axis=1, tiled=True),
    )
    out_bf, grad_q_own, grad_k_own, grad_v_own = tuple(
        (part.reshape(tok_rows, HEADS, HD) for part in back_rows)
    )
    attn_out = (
        (head_gate[None, :, None] * lax.optimization_barrier(out_bf).astype(jnp.float32))
        .astype(jnp.bfloat16)
        .reshape(tok_rows, row_width)
    )
    back_query, back_key, back_value = send_back(
        as_blocks(grad_q_own, back_slot),
        as_blocks(grad_k_own, back_slot),
        as_blocks(grad_v_own, back_slot),
    )
    grad_queries = back_query[loader_slot].reshape(tok_rows, row_width)
    grad_keys = back_key[loader_slot].reshape(tok_rows, row_width)
    grad_values = back_value[loader_slot].reshape(tok_rows, row_width)
    return (attn_out, grad_queries, grad_keys, grad_values)


def dot_nn(left, right):
    return lax.dot_general(left, right, (((1,), (0,)), ((), ())), preferred_element_type=F32)


def dot_nt(left, right):
    return lax.dot_general(left, right, (((1,), (1,)), ((), ())), preferred_element_type=F32)


def dot_tn(left, right):
    return lax.dot_general(left, right, (((0,), (0,)), ((), ())), preferred_element_type=F32)


def iota(shape, axis):
    return lax.broadcasted_iota(jnp.int32, shape, axis)


def fused_kernel(
    n_dp,
    n_sp,
    block_rows,
    heads_dev,
    length_ref,
    plan_ref,
    bin_ref,
    table_ref,
    source_ref,
    q_ref,
    k_ref,
    v_ref,
    cot_ref,
    out_ref,
    gq_ref,
    gk_ref,
    gv_ref,
    load_buf,
    send_buf,
    recv_buf,
    cot_buf,
    grad_buf,
    back_buf,
    out_buf,
    oback_buf,
    order_buf,
    unorder_buf,
    pick_buf,
    stage_buf,
    load_sem,
    send_sem,
    recv_sem,
    gsend_sem,
    back_sem,
    csend_sem,
    crecv_sem,
    osend_sem,
    orecv_sem,
    local_sem,
    store_sem,
):
    n = n_dp * n_sp
    chunk = n_sp * block_rows
    tok = q_ref.shape[0]
    group_tok = tok * n_sp
    group_blocks = group_tok // block_rows
    group = lax.axis_index("dp")
    part = lax.axis_index("sp")
    me = group * n_sp + part
    my_part_rows = pl.ds(pl.multiple_of(part * tok, tok), tok)

    def load(j, carry):
        for part_to in range(n_sp):
            columns = pl.ds(pl.multiple_of((part_to * heads_dev + j) * HD, HD), HD)
            for which, ref in enumerate((q_ref, k_ref, v_ref)):
                pltpu.make_async_copy(
                    ref.at[:, columns], load_buf.at[j, part_to, which], load_sem.at[j]
                ).start()
        return carry

    barrier = pltpu.get_barrier_semaphore()
    load(0, 0)

    def greet(i, carry):
        peer = (me + 1 + i) % n
        pl.semaphore_signal(
            barrier, inc=1, device_id=(peer // n_sp, peer % n_sp), device_id_type=MESH
        )
        return carry

    lax.fori_loop(0, n - 1, greet, 0)
    lax.fori_loop(1, heads_dev, load, 0)

    source = source_ref[...]
    loader_of = source // n
    mine = jnp.where(loader_of == me, source % n, 0)
    spread = jnp.broadcast_to(mine[:, None, :], (n_dp, chunk, group_blocks)).reshape(
        n_dp * chunk, group_blocks
    )
    row_part = (iota((n_dp * chunk, group_blocks), 0) // block_rows) % n_sp
    col_part = iota((n_dp * chunk, group_blocks), 1) // n
    slot = jnp.sum(jnp.where(row_part == col_part, spread, 0), axis=1, keepdims=True)
    pick_row = slot * block_rows + iota((n_dp * chunk, 1), 0) % block_rows
    pick_buf[...] = jnp.where(iota((n_dp * chunk, tok), 1) == pick_row, 1.0, 0.0).astype(BF16)

    def wait_bytes(ref, sem):
        pltpu.make_async_copy(ref, ref, sem).wait()

    def prepare(j):
        wait_bytes(load_buf.at[j], load_sem.at[j])
        for part_to in range(n_sp):
            head = part_to * heads_dev + j
            for which in range(3):
                send_buf[head, :, which] = (
                    dot_nn(pick_buf[...], load_buf[j, part_to, which])
                    .astype(BF16)
                    .reshape(n_dp, chunk, HD)
                )

    def peer_at(i):
        turn = i + (i + n - 3) // (n - 1)
        quarter = n // 4
        outer = (me // quarter + 6 - turn % 4) % 4
        peer = outer * quarter + (me % quarter + turn // 4) % quarter
        return peer // n_sp, peer % n_sp

    def forward(j):
        def one(i, carry):
            to_group, to_part = peer_at(i)
            pltpu.make_async_remote_copy(
                src_ref=send_buf.at[to_part * heads_dev + j, to_group],
                dst_ref=recv_buf.at[j, me],
                send_sem=send_sem.at[j],
                recv_sem=recv_sem.at[j],
                device_id=(to_group, to_part),
                device_id_type=MESH,
            ).start()
            return carry

        lax.fori_loop(0, n - 1, one, 0)
        pltpu.make_async_copy(
            send_buf.at[part * heads_dev + j, group],
            recv_buf.at[j, me],
            local_sem.at[j],
        ).start()

    def backward(j):
        def one(i, carry):
            to_group, to_part = peer_at(i)
            to = to_group * n_sp + to_part
            pltpu.make_async_remote_copy(
                src_ref=grad_buf.at[j, to],
                dst_ref=back_buf.at[part * heads_dev + j, group],
                send_sem=gsend_sem.at[j],
                recv_sem=back_sem.at[j],
                device_id=(to_group, to_part),
                device_id_type=MESH,
            ).start()
            return carry

        lax.fori_loop(0, n - 1, one, 0)
        pltpu.make_async_copy(
            grad_buf.at[j, me],
            back_buf.at[part * heads_dev + j, group],
            local_sem.at[heads_dev + j],
        ).start()

        for step in range(1, n_sp):
            to_part = (part + step) % n_sp
            pltpu.make_async_remote_copy(
                src_ref=out_buf.at[j, pl.ds(pl.multiple_of(to_part * tok, tok), tok), :],
                dst_ref=oback_buf.at[part * heads_dev + j],
                send_sem=osend_sem.at[j],
                recv_sem=orecv_sem.at[j],
                device_id=(group, to_part),
                device_id_type=MESH,
            ).start()
        pltpu.make_async_copy(
            out_buf.at[j, my_part_rows, :],
            oback_buf.at[part * heads_dev + j],
            local_sem.at[2 * heads_dev + j],
        ).start()

    width = heads_dev * HD
    prepare(0)
    pl.semaphore_wait(barrier, n - 1)
    forward(0)
    for step in range(1, n_sp):
        to_part = (part + step) % n_sp
        pltpu.make_async_remote_copy(
            src_ref=cot_ref.at[:, pl.ds(pl.multiple_of(to_part * width, HD), width)],
            dst_ref=cot_buf.at[my_part_rows, :],
            send_sem=csend_sem,
            recv_sem=crecv_sem,
            device_id=(group, to_part),
            device_id_type=MESH,
        ).start()
    pltpu.make_async_copy(
        cot_ref.at[:, pl.ds(pl.multiple_of(part * width, HD), width)],
        cot_buf.at[my_part_rows, :],
        local_sem.at[3 * heads_dev],
    ).start()

    def send_more(j, carry):
        prepare(j)
        forward(j)
        return carry

    lax.fori_loop(1, heads_dev, send_more, 0)

    group_len = jnp.int32(0)
    group_bin = jnp.int32(0)
    for sample in range(n_dp):
        picked = plan_ref[sample] == group
        group_len += jnp.where(picked, length_ref[sample], 0)
        group_bin += jnp.where(picked, bin_ref[sample], 0)

    loader_row = (source_ref[pl.ds(group, 1), :] // n).astype(F32)
    widen = jnp.where(
        iota((group_blocks, group_tok), 0) == iota((group_blocks, group_tok), 1) // block_rows,
        1.0,
        0.0,
    ).astype(BF16)
    place = iota((1, group_tok), 1)
    lane_loader = dot_nn(
        jnp.broadcast_to(loader_row, (16, group_blocks)).astype(BF16), widen
    )[0:1].astype(jnp.int32)
    lane_row = lane_loader * chunk + (place // tok) * block_rows + place % block_rows
    col_loader = jnp.sum(
        jnp.where(
            iota((group_tok, group_blocks), 1) == iota((group_tok, group_blocks), 0) // block_rows,
            loader_row,
            0.0,
        ),
        axis=1,
        keepdims=True,
    ).astype(jnp.int32)
    col_place = iota((group_tok, 1), 0)
    col_row = col_loader * chunk + (col_place // tok) * block_rows + col_place % block_rows
    square = (group_tok, group_tok)
    order = jnp.where(iota(square, 0) == lane_row, 1.0, 0.0)
    unorder = jnp.where(iota(square, 1) == col_row, 1.0, 0.0)
    order_buf[...] = order.astype(BF16)
    unorder_buf[...] = unorder.astype(BF16)
    key_live = jnp.sum(jnp.where(place < group_len, order, 0.0), axis=1, keepdims=True)
    query_live = jnp.sum(jnp.where(col_place < group_len, unorder, 0.0), axis=0, keepdims=True)

    wait_bytes(cot_buf.at[pl.ds(0, (n_sp - 1) * tok), :], crecv_sem)
    wait_bytes(cot_buf.at[my_part_rows, :], local_sem.at[3 * heads_dev])

    scale = HD ** (-0.5)

    def one_head(j, carry):
        gate = table_ref[group_bin, part * heads_dev + j]
        columns = pl.ds(pl.multiple_of(j * HD, HD), HD)
        d_out = (gate * dot_nn(order_buf[...], cot_buf[:, columns])).astype(BF16)
        wait_bytes(recv_buf.at[j, pl.ds(0, n - 1)], recv_sem.at[j])
        wait_bytes(recv_buf.at[j, me], local_sem.at[j])
        query, key, value = (recv_buf[j, :, at].reshape(group_tok, HD) for at in range(3))
        scores = dot_nt(key, query) * scale
        scores = jnp.where(key_live > 0.5, scores, -1e30)
        top = jnp.max(scores, axis=0, keepdims=True)
        shifted = jnp.exp(scores - top)
        total = jnp.sum(shifted, axis=0, keepdims=True)
        attend = shifted * (query_live / total)
        attend_bf = attend.astype(BF16)
        grad_attend = dot_nt(value, d_out)
        row_dot = jnp.sum(attend_bf.astype(F32) * grad_attend, axis=0, keepdims=True)
        grad_scores = (attend * (grad_attend - row_dot) * scale).astype(BF16)
        grad_buf[j, :, 2] = dot_nn(attend_bf, d_out).astype(BF16).reshape(n, chunk, HD)
        grad_buf[j, :, 1] = dot_nn(grad_scores, query).astype(BF16).reshape(n, chunk, HD)
        grad_buf[j, :, 0] = dot_tn(grad_scores, key).astype(BF16).reshape(n, chunk, HD)
        output = dot_tn(attend_bf, value).astype(BF16)
        gated = (gate * output.astype(F32)).astype(BF16)
        out_buf[j] = dot_nn(unorder_buf[...], gated).astype(BF16)
        backward(j)
        return carry

    lax.fori_loop(0, heads_dev, one_head, 0)

    def collect(j, carry):
        wait_bytes(recv_buf.at[j, pl.ds(0, n - 1)], back_sem.at[j])
        wait_bytes(recv_buf.at[j, me], local_sem.at[heads_dev + j])
        wait_bytes(out_buf.at[j, pl.ds(0, (n_sp - 1) * tok), :], orecv_sem.at[j])
        wait_bytes(out_buf.at[j, my_part_rows, :], local_sem.at[2 * heads_dev + j])
        for part_from in range(n_sp):
            head = part_from * heads_dev + j
            columns = pl.ds(pl.multiple_of(head * HD, HD), HD)
            pltpu.make_async_copy(
                oback_buf.at[head], out_ref.at[:, columns], store_sem.at[0]
            ).start()
            for which, ref in enumerate((gq_ref, gk_ref, gv_ref)):
                arrived = back_buf[head, :, which].reshape(n_dp * chunk, HD)
                stage_buf[head, which] = dot_tn(pick_buf[...], arrived).astype(BF16)
                pltpu.make_async_copy(
                    stage_buf.at[head, which], ref.at[:, columns], store_sem.at[1 + which]
                ).start()
        return carry

    lax.fori_loop(0, heads_dev, collect, 0)

    def drain(j, carry):
        wait_bytes(recv_buf.at[j, pl.ds(0, n - 1)], send_sem.at[j])
        wait_bytes(recv_buf.at[j, pl.ds(0, n - 1)], gsend_sem.at[j])
        wait_bytes(out_buf.at[j, pl.ds(0, (n_sp - 1) * tok), :], osend_sem.at[j])
        return carry

    lax.fori_loop(0, heads_dev, drain, 0)
    wait_bytes(cot_buf.at[pl.ds(0, (n_sp - 1) * tok), :], csend_sem)
    for which in range(4):
        wait_bytes(oback_buf, store_sem.at[which])


def place_kernel(*refs):
    sources, targets, held, in_sems, out_sems = refs[:4], refs[4:8], refs[8], refs[9], refs[10]
    rows = 32
    pieces = sources[0].shape[0] // rows

    def copies_of(which, piece):
        at = pl.ds(piece * rows, rows)
        index = which * pieces + piece
        return (
            pltpu.make_async_copy(
                sources[which].at[at, :], held.at[which, at, :], in_sems.at[index]
            ),
            pltpu.make_async_copy(
                held.at[which, at, :], targets[which].at[at, :], out_sems.at[index]
            ),
        )

    pairs = [copies_of(which, piece) for which in range(4) for piece in range(pieces)]
    for inward, _ in pairs:
        inward.start()
    for inward, outward in pairs:
        inward.wait()
        outward.start()
    for _, outward in pairs:
        outward.wait()


def place_outputs(results):
    hbm = pl.BlockSpec(memory_space=pltpu.HBM)
    pieces = 4 * (results[0].shape[0] // 32)
    return pl.pallas_call(
        place_kernel,
        out_shape=[jax.ShapeDtypeStruct(result.shape, BF16) for result in results],
        in_specs=[hbm] * 4,
        out_specs=[hbm] * 4,
        scratch_shapes=[
            pltpu.VMEM((4,) + results[0].shape, BF16),
            pltpu.SemaphoreType.DMA((pieces,)),
            pltpu.SemaphoreType.DMA((pieces,)),
        ],
        compiler_params=pltpu.CompilerParams(vmem_limit_bytes=VMEM_GRANT),
        name="place_outputs",
    )(*results)


def fused(
    n_dp,
    n_sp,
    queries,
    key_rows,
    value_rows,
    cotangent,
    lengths,
    sample_plan,
    guide_bins,
    guide_table,
    block_source,
):
    tok, row_width = queries.shape
    n = n_dp * n_sp
    heads_dev = HEADS // n_sp
    group_tok = tok * n_sp
    smem = pl.BlockSpec(memory_space=pltpu.SMEM)
    vmem = pl.BlockSpec(memory_space=pltpu.VMEM)
    hbm = pl.BlockSpec(memory_space=pltpu.HBM)
    flops = 2 * 8 * heads_dev * group_tok * group_tok * HD
    return pl.pallas_call(
        functools.partial(fused_kernel, n_dp, n_sp, tok // n, heads_dev),
        out_shape=[jax.ShapeDtypeStruct((tok, row_width), BF16)] * 4,
        in_specs=[smem] * 4 + [vmem] + [hbm] * 4,
        out_specs=[hbm] * 4,
        scratch_shapes=[
            pltpu.VMEM((heads_dev, n_sp, 3, tok, HD), BF16),
            pltpu.VMEM((HEADS, n_dp, 3, tok // n_dp, HD), BF16),
            pltpu.VMEM((heads_dev, n, 3, group_tok // n, HD), BF16),
            pltpu.VMEM((group_tok, heads_dev * HD), BF16),
            pltpu.VMEM((heads_dev, n, 3, group_tok // n, HD), BF16),
            pltpu.VMEM((HEADS, n_dp, 3, tok // n_dp, HD), BF16),
            pltpu.VMEM((heads_dev, group_tok, HD), BF16),
            pltpu.VMEM((HEADS, tok, HD), BF16),
            pltpu.VMEM((group_tok, group_tok), BF16),
            pltpu.VMEM((group_tok, group_tok), BF16),
            pltpu.VMEM((tok, tok), BF16),
            pltpu.VMEM((HEADS, 3, tok, HD), BF16),
            pltpu.SemaphoreType.DMA((heads_dev,)),
            pltpu.SemaphoreType.DMA((heads_dev,)),
            pltpu.SemaphoreType.DMA((heads_dev,)),
            pltpu.SemaphoreType.DMA((heads_dev,)),
            pltpu.SemaphoreType.DMA((heads_dev,)),
            pltpu.SemaphoreType.DMA,
            pltpu.SemaphoreType.DMA,
            pltpu.SemaphoreType.DMA((heads_dev,)),
            pltpu.SemaphoreType.DMA((heads_dev,)),
            pltpu.SemaphoreType.DMA((3 * heads_dev + 1,)),
            pltpu.SemaphoreType.DMA((4,)),
        ],
        compiler_params=pltpu.CompilerParams(
            collective_id=0, has_side_effects=True, vmem_limit_bytes=VMEM_GRANT
        ),
        cost_estimate=pl.CostEstimate(
            flops=flops, bytes_accessed=16 * tok * row_width, transcendentals=0
        ),
        name="routed_attention",
    )(
        lengths,
        sample_plan,
        guide_bins,
        guide_table,
        block_source.reshape(n_dp, block_source.shape[0] // n_dp),
        queries,
        key_rows,
        value_rows,
        cotangent,
    )


def chosen(*arrays):
    n_dp, n_sp = lax.axis_size("dp"), lax.axis_size("sp")
    tok = arrays[0].shape[0]
    block_rows = tok // (n_dp * n_sp)
    if (n_sp * block_rows) % 16 == 0 and HEADS % n_sp == 0:
        return place_outputs(fused(n_dp, n_sp, *arrays))
    return per_device(*arrays)


def solution(mesh):
    placed = (
        P(("dp", "sp"), None),
        P(("dp", "sp"), None),
        P(("dp", "sp"), None),
        P(("dp", "sp"), None),
        P(),
        P(),
        P(),
        P(),
        P(),
    )
    return jax.shard_map(
        chosen,
        mesh=mesh,
        in_specs=placed,
        out_specs=(
            P(("dp", "sp"), None),
            P(("dp", "sp"), None),
            P(("dp", "sp"), None),
            P(("dp", "sp"), None),
        ),
        check_vma=False,
    )
```

```python
import functools

import jax
import jax.numpy as jnp
from jax import lax
from jax.experimental import pallas as pl
from jax.experimental.pallas import tpu as pltpu
from jax.sharding import PartitionSpec as P

HEADS = 20
HD = 128
MESH = pl.DeviceIdType.MESH
VMEM_GRANT = 62 * 1024 * 1024
F32 = jnp.float32
BF16 = jnp.bfloat16


def head_pass(query_head, key_head, value_head, grad_head, query_live, key_live):
    scores = jnp.dot(query_head, key_head.T, preferred_element_type=jnp.float32) * HD ** (-0.5)
    masked = jnp.where(key_live[None, :], scores, -1e30)
    top_score = jnp.max(masked, axis=1, keepdims=True)
    shifted_exp = jnp.where(key_live[None, :], jnp.exp(masked - top_score), 0.0)
    row_total = jnp.sum(shifted_exp, axis=1, keepdims=True)
    attend = jnp.where(query_live[:, None], shifted_exp / row_total, 0.0)
    attend_bf = attend.astype(jnp.bfloat16)
    output = jnp.dot(attend_bf, value_head, preferred_element_type=jnp.float32)
    grad_attend = jnp.dot(grad_head, value_head.T, preferred_element_type=jnp.float32)
    row_dot = jnp.sum(grad_head.astype(jnp.float32) * output, axis=1, keepdims=True)
    grad_scores = (attend * (grad_attend - row_dot) * HD ** (-0.5)).astype(jnp.bfloat16)
    grad_query = jnp.dot(grad_scores, key_head, preferred_element_type=jnp.float32)
    grad_key = jnp.dot(grad_scores.T, query_head, preferred_element_type=jnp.float32)
    grad_value = jnp.dot(attend_bf.T, grad_head, preferred_element_type=jnp.float32)
    return (output, grad_query, grad_key, grad_value)


def head_stack(query_part, key_part, value_part, grad_part, query_live, key_live):

    def one_head(head_items):
        return head_pass(
            head_items[0], head_items[1], head_items[2], head_items[3], query_live, key_live
        )

    stacked = tuple(
        (jnp.moveaxis(source, 1, 0) for source in (query_part, key_part, value_part, grad_part))
    )
    return lax.map(one_head, stacked)


def dispatch(first, second, third):
    return (
        lax.all_to_all(first, ("dp", "sp"), split_axis=0, concat_axis=0, tiled=True),
        lax.all_to_all(second, ("dp", "sp"), split_axis=0, concat_axis=0, tiled=True),
        lax.all_to_all(third, ("dp", "sp"), split_axis=0, concat_axis=0, tiled=True),
    )


def send_back(first, second, third):
    return (
        lax.all_to_all(first, ("dp", "sp"), split_axis=0, concat_axis=0, tiled=True),
        lax.all_to_all(second, ("dp", "sp"), split_axis=0, concat_axis=0, tiled=True),
        lax.all_to_all(third, ("dp", "sp"), split_axis=0, concat_axis=0, tiled=True),
    )


def per_device(
    queries,
    key_rows,
    value_rows,
    cotangent,
    lengths,
    sample_plan,
    guide_bins,
    guide_table,
    block_source,
):
    n_dp = lax.axis_size("dp")
    n_sp = lax.axis_size("sp")
    loaders = n_dp * n_sp
    tok_rows = queries.shape[0]
    row_width = queries.shape[1]
    block_rows = tok_rows // loaders
    device_index = lax.axis_index("dp") * n_sp + lax.axis_index("sp")
    table = block_source.reshape(loaders, loaders)
    sources = table[device_index] // loaders
    send_slot = jnp.sum(jnp.where(table // loaders == device_index, table % loaders, 0), axis=1)
    slot_index = jnp.arange(loaders, dtype=jnp.int32)
    back_slot = jnp.sum(
        jnp.where(sources[None, :] == slot_index[:, None], slot_index[None, :], 0), axis=1
    )
    loader_slot = jnp.sum(
        jnp.where(send_slot[None, :] == slot_index[:, None], slot_index[None, :], 0), axis=1
    )

    def as_blocks(source, order):
        return source.reshape(loaders, block_rows, row_width)[order]

    recv_query, recv_key, recv_value = dispatch(
        as_blocks(queries, send_slot),
        as_blocks(key_rows, send_slot),
        as_blocks(value_rows, send_slot),
    )
    query_own = recv_query[sources].reshape(tok_rows, HEADS, HD)
    key_own = recv_key[sources].reshape(tok_rows, HEADS, HD)
    value_own = recv_value[sources].reshape(tok_rows, HEADS, HD)
    group_index = lax.axis_index("dp")
    picked = sample_plan == group_index
    group_len = jnp.sum(jnp.where(picked, lengths, 0))
    group_bin = jnp.sum(jnp.where(picked, guide_bins, 0))
    bin_match = jnp.arange(guide_table.shape[0], dtype=jnp.int32) == group_bin
    head_gate = jnp.sum(jnp.where(bin_match[:, None], guide_table, 0.0), axis=0)
    grad_own = (
        head_gate[None, :, None] * cotangent.reshape(tok_rows, HEADS, HD).astype(jnp.float32)
    ).astype(jnp.bfloat16)
    heads_dev = HEADS // n_sp
    split_shape = (tok_rows, n_sp, heads_dev, HD)
    group_items = (
        lax.all_to_all(
            query_own.reshape(split_shape), "sp", split_axis=1, concat_axis=0, tiled=True
        ),
        lax.all_to_all(key_own.reshape(split_shape), "sp", split_axis=1, concat_axis=0, tiled=True),
        lax.all_to_all(
            value_own.reshape(split_shape), "sp", split_axis=1, concat_axis=0, tiled=True
        ),
        lax.all_to_all(
            grad_own.reshape(split_shape), "sp", split_axis=1, concat_axis=0, tiled=True
        ),
    )
    flat_items = tuple((item[:, 0] for item in group_items))
    live_rows = jnp.arange(flat_items[0].shape[0], dtype=jnp.int32) < group_len
    results = head_stack(
        flat_items[0], flat_items[1], flat_items[2], flat_items[3], live_rows, live_rows
    )
    out_heads, gq_heads, gk_heads, gv_heads = tuple(
        (jnp.moveaxis(result, 0, 1)[:, None].astype(jnp.bfloat16) for result in results)
    )
    back_rows = (
        lax.all_to_all(out_heads, "sp", split_axis=0, concat_axis=1, tiled=True),
        lax.all_to_all(gq_heads, "sp", split_axis=0, concat_axis=1, tiled=True),
        lax.all_to_all(gk_heads, "sp", split_axis=0, concat_axis=1, tiled=True),
        lax.all_to_all(gv_heads, "sp", split_axis=0, concat_axis=1, tiled=True),
    )
    out_bf, grad_q_own, grad_k_own, grad_v_own = tuple(
        (part.reshape(tok_rows, HEADS, HD) for part in back_rows)
    )
    attn_out = (
        (head_gate[None, :, None] * lax.optimization_barrier(out_bf).astype(jnp.float32))
        .astype(jnp.bfloat16)
        .reshape(tok_rows, row_width)
    )
    back_query, back_key, back_value = send_back(
        as_blocks(grad_q_own, back_slot),
        as_blocks(grad_k_own, back_slot),
        as_blocks(grad_v_own, back_slot),
    )
    grad_queries = back_query[loader_slot].reshape(tok_rows, row_width)
    grad_keys = back_key[loader_slot].reshape(tok_rows, row_width)
    grad_values = back_value[loader_slot].reshape(tok_rows, row_width)
    return (attn_out, grad_queries, grad_keys, grad_values)


def dot_nn(left, right):
    return lax.dot_general(left, right, (((1,), (0,)), ((), ())), preferred_element_type=F32)


def dot_nt(left, right):
    return lax.dot_general(left, right, (((1,), (1,)), ((), ())), preferred_element_type=F32)


def dot_tn(left, right):
    return lax.dot_general(left, right, (((0,), (0,)), ((), ())), preferred_element_type=F32)


def iota(shape, axis):
    return lax.broadcasted_iota(jnp.int32, shape, axis)


def fused_kernel(
    n_dp,
    n_sp,
    block_rows,
    heads_dev,
    length_ref,
    plan_ref,
    bin_ref,
    table_ref,
    source_ref,
    q_ref,
    k_ref,
    v_ref,
    cot_ref,
    out_ref,
    gq_ref,
    gk_ref,
    gv_ref,
    load_buf,
    send_buf,
    recv_buf,
    cot_buf,
    grad_buf,
    back_buf,
    out_buf,
    oback_buf,
    order_buf,
    unorder_buf,
    pick_buf,
    stage_buf,
    load_sem,
    send_sem,
    recv_sem,
    gsend_sem,
    back_sem,
    csend_sem,
    crecv_sem,
    osend_sem,
    orecv_sem,
    local_sem,
    store_sem,
):
    n = n_dp * n_sp
    chunk = n_sp * block_rows
    tok = q_ref.shape[0]
    group_tok = tok * n_sp
    group_blocks = group_tok // block_rows
    group = lax.axis_index("dp")
    part = lax.axis_index("sp")
    me = group * n_sp + part
    my_part_rows = pl.ds(pl.multiple_of(part * tok, tok), tok)

    def load(j, carry):
        for part_to in range(n_sp):
            columns = pl.ds(pl.multiple_of((part_to * heads_dev + j) * HD, HD), HD)
            for which, ref in enumerate((q_ref, k_ref, v_ref)):
                pltpu.make_async_copy(
                    ref.at[:, columns], load_buf.at[j, part_to, which], load_sem.at[j]
                ).start()
        return carry

    barrier = pltpu.get_barrier_semaphore()
    load(0, 0)

    def greet(i, carry):
        peer = (me + 1 + i) % n
        pl.semaphore_signal(
            barrier, inc=1, device_id=(peer // n_sp, peer % n_sp), device_id_type=MESH
        )
        return carry

    lax.fori_loop(0, n - 1, greet, 0)
    lax.fori_loop(1, heads_dev, load, 0)

    source = source_ref[...]
    loader_of = source // n
    mine = jnp.where(loader_of == me, source % n, 0)
    spread = jnp.broadcast_to(mine[:, None, :], (n_dp, chunk, group_blocks)).reshape(
        n_dp * chunk, group_blocks
    )
    row_part = (iota((n_dp * chunk, group_blocks), 0) // block_rows) % n_sp
    col_part = iota((n_dp * chunk, group_blocks), 1) // n
    slot = jnp.sum(jnp.where(row_part == col_part, spread, 0), axis=1, keepdims=True)
    pick_row = slot * block_rows + iota((n_dp * chunk, 1), 0) % block_rows
    pick_buf[...] = jnp.where(iota((n_dp * chunk, tok), 1) == pick_row, 1.0, 0.0).astype(BF16)

    def wait_bytes(ref, sem):
        pltpu.make_async_copy(ref, ref, sem).wait()

    def prepare(j):
        wait_bytes(load_buf.at[j], load_sem.at[j])
        for part_to in range(n_sp):
            head = part_to * heads_dev + j
            for which in range(3):
                send_buf[head, :, which] = (
                    dot_nn(pick_buf[...], load_buf[j, part_to, which])
                    .astype(BF16)
                    .reshape(n_dp, chunk, HD)
                )

    def peer_at(i):
        turn = i + (i + n - 3) // (n - 1)
        quarter = n // 4
        outer = (me // quarter + 6 - turn % 4) % 4
        peer = outer * quarter + (me % quarter + turn // 4) % quarter
        return peer // n_sp, peer % n_sp

    def forward(at, first, size):
        def one(i, carry):
            to_group, to_part = peer_at(i)
            pltpu.make_async_remote_copy(
                src_ref=send_buf.at[pl.ds(to_part * heads_dev + first, size), to_group],
                dst_ref=recv_buf.at[pl.ds(first, size), me],
                send_sem=send_sem.at[at],
                recv_sem=recv_sem.at[at],
                device_id=(to_group, to_part),
                device_id_type=MESH,
            ).start()
            return carry

        lax.fori_loop(0, n - 1, one, 0)
        pltpu.make_async_copy(
            send_buf.at[pl.ds(part * heads_dev + first, size), group],
            recv_buf.at[pl.ds(first, size), me],
            local_sem.at[at],
        ).start()

    def backward(at, first, size):
        def one(i, carry):
            to_group, to_part = peer_at(i)
            to = to_group * n_sp + to_part
            pltpu.make_async_remote_copy(
                src_ref=grad_buf.at[pl.ds(first, size), to],
                dst_ref=back_buf.at[pl.ds(part * heads_dev + first, size), group],
                send_sem=gsend_sem.at[at],
                recv_sem=back_sem.at[at],
                device_id=(to_group, to_part),
                device_id_type=MESH,
            ).start()
            return carry

        lax.fori_loop(0, n - 1, one, 0)
        pltpu.make_async_copy(
            grad_buf.at[pl.ds(first, size), me],
            back_buf.at[pl.ds(part * heads_dev + first, size), group],
            local_sem.at[heads_dev + at],
        ).start()

        for step in range(1, n_sp):
            to_part = (part + step) % n_sp
            pltpu.make_async_remote_copy(
                src_ref=out_buf.at[
                    pl.ds(first, size), pl.ds(pl.multiple_of(to_part * tok, tok), tok), :
                ],
                dst_ref=oback_buf.at[pl.ds(part * heads_dev + first, size)],
                send_sem=osend_sem.at[at],
                recv_sem=orecv_sem.at[at],
                device_id=(group, to_part),
                device_id_type=MESH,
            ).start()
        pltpu.make_async_copy(
            out_buf.at[pl.ds(first, size), my_part_rows, :],
            oback_buf.at[pl.ds(part * heads_dev + first, size)],
            local_sem.at[2 * heads_dev + at],
        ).start()

    width = heads_dev * HD
    batches = [
        (at, first, min(2, heads_dev - first)) for at, first in enumerate(range(0, heads_dev, 2))
    ]

    def prepare_batch(first, size):
        def one(j, carry):
            prepare(j)
            return carry

        lax.fori_loop(first, first + size, one, 0)

    prepare_batch(0, batches[0][2])
    pl.semaphore_wait(barrier, n - 1)
    forward(*batches[0])
    for step in range(1, n_sp):
        to_part = (part + step) % n_sp
        pltpu.make_async_remote_copy(
            src_ref=cot_ref.at[:, pl.ds(pl.multiple_of(to_part * width, HD), width)],
            dst_ref=cot_buf.at[my_part_rows, :],
            send_sem=csend_sem,
            recv_sem=crecv_sem,
            device_id=(group, to_part),
            device_id_type=MESH,
        ).start()
    pltpu.make_async_copy(
        cot_ref.at[:, pl.ds(pl.multiple_of(part * width, HD), width)],
        cot_buf.at[my_part_rows, :],
        local_sem.at[3 * heads_dev],
    ).start()

    for at, first, size in batches[1:]:
        prepare_batch(first, size)
        forward(at, first, size)

    group_len = jnp.int32(0)
    group_bin = jnp.int32(0)
    for sample in range(n_dp):
        picked = plan_ref[sample] == group
        group_len += jnp.where(picked, length_ref[sample], 0)
        group_bin += jnp.where(picked, bin_ref[sample], 0)

    loader_row = (source_ref[pl.ds(group, 1), :] // n).astype(F32)
    widen = jnp.where(
        iota((group_blocks, group_tok), 0) == iota((group_blocks, group_tok), 1) // block_rows,
        1.0,
        0.0,
    ).astype(BF16)
    place = iota((1, group_tok), 1)
    lane_loader = dot_nn(
        jnp.broadcast_to(loader_row, (16, group_blocks)).astype(BF16), widen
    )[0:1].astype(jnp.int32)
    lane_row = lane_loader * chunk + (place // tok) * block_rows + place % block_rows
    col_loader = jnp.sum(
        jnp.where(
            iota((group_tok, group_blocks), 1) == iota((group_tok, group_blocks), 0) // block_rows,
            loader_row,
            0.0,
        ),
        axis=1,
        keepdims=True,
    ).astype(jnp.int32)
    col_place = iota((group_tok, 1), 0)
    col_row = col_loader * chunk + (col_place // tok) * block_rows + col_place % block_rows
    square = (group_tok, group_tok)
    order = jnp.where(iota(square, 0) == lane_row, 1.0, 0.0)
    unorder = jnp.where(iota(square, 1) == col_row, 1.0, 0.0)
    order_buf[...] = order.astype(BF16)
    unorder_buf[...] = unorder.astype(BF16)
    key_live = jnp.sum(jnp.where(place < group_len, order, 0.0), axis=1, keepdims=True)
    query_live = jnp.sum(jnp.where(col_place < group_len, unorder, 0.0), axis=0, keepdims=True)

    wait_bytes(cot_buf.at[pl.ds(0, (n_sp - 1) * tok), :], crecv_sem)
    wait_bytes(cot_buf.at[my_part_rows, :], local_sem.at[3 * heads_dev])

    scale = HD ** (-0.5)

    def one_head(j, carry):
        gate = table_ref[group_bin, part * heads_dev + j]
        columns = pl.ds(pl.multiple_of(j * HD, HD), HD)
        d_out = (gate * dot_nn(order_buf[...], cot_buf[:, columns])).astype(BF16)
        for at, first, size in batches:

            @pl.when(j == first)
            def _():
                heads = pl.ds(first, size)
                wait_bytes(recv_buf.at[heads, pl.ds(0, n - 1)], recv_sem.at[at])
                wait_bytes(recv_buf.at[heads, me], local_sem.at[at])

        query, key, value = (recv_buf[j, :, at].reshape(group_tok, HD) for at in range(3))
        scores = dot_nt(key, query) * scale
        scores = jnp.where(key_live > 0.5, scores, -1e30)
        top = jnp.max(scores, axis=0, keepdims=True)
        shifted = jnp.exp(scores - top)
        total = jnp.sum(shifted, axis=0, keepdims=True)
        attend = shifted * (query_live / total)
        attend_bf = attend.astype(BF16)
        grad_attend = dot_nt(value, d_out)
        row_dot = jnp.sum(attend_bf.astype(F32) * grad_attend, axis=0, keepdims=True)
        grad_scores = (attend * (grad_attend - row_dot) * scale).astype(BF16)
        grad_buf[j, :, 2] = dot_nn(attend_bf, d_out).astype(BF16).reshape(n, chunk, HD)
        grad_buf[j, :, 1] = dot_nn(grad_scores, query).astype(BF16).reshape(n, chunk, HD)
        grad_buf[j, :, 0] = dot_tn(grad_scores, key).astype(BF16).reshape(n, chunk, HD)
        output = dot_tn(attend_bf, value).astype(BF16)
        gated = (gate * output.astype(F32)).astype(BF16)
        out_buf[j] = dot_nn(unorder_buf[...], gated).astype(BF16)
        for at, first, size in batches:

            @pl.when(j == first + size - 1)
            def _():
                backward(at, first, size)

        return carry

    lax.fori_loop(0, heads_dev, one_head, 0)

    def collect(j, carry):
        for at, first, size in batches:

            @pl.when(j == first)
            def _():
                heads = pl.ds(first, size)
                wait_bytes(recv_buf.at[heads, pl.ds(0, n - 1)], back_sem.at[at])
                wait_bytes(recv_buf.at[heads, me], local_sem.at[heads_dev + at])
                wait_bytes(out_buf.at[heads, pl.ds(0, (n_sp - 1) * tok), :], orecv_sem.at[at])
                wait_bytes(out_buf.at[heads, my_part_rows, :], local_sem.at[2 * heads_dev + at])

        for part_from in range(n_sp):
            head = part_from * heads_dev + j
            columns = pl.ds(pl.multiple_of(head * HD, HD), HD)
            pltpu.make_async_copy(
                oback_buf.at[head], out_ref.at[:, columns], store_sem.at[0]
            ).start()
            for which, ref in enumerate((gq_ref, gk_ref, gv_ref)):
                arrived = back_buf[head, :, which].reshape(n_dp * chunk, HD)
                stage_buf[head, which] = dot_tn(pick_buf[...], arrived).astype(BF16)
                pltpu.make_async_copy(
                    stage_buf.at[head, which], ref.at[:, columns], store_sem.at[1 + which]
                ).start()
        return carry

    lax.fori_loop(0, heads_dev, collect, 0)

    for at, first, size in batches:
        heads = pl.ds(first, size)
        wait_bytes(recv_buf.at[heads, pl.ds(0, n - 1)], send_sem.at[at])
        wait_bytes(recv_buf.at[heads, pl.ds(0, n - 1)], gsend_sem.at[at])
        wait_bytes(out_buf.at[heads, pl.ds(0, (n_sp - 1) * tok), :], osend_sem.at[at])
    wait_bytes(cot_buf.at[pl.ds(0, (n_sp - 1) * tok), :], csend_sem)
    for which in range(4):
        wait_bytes(oback_buf, store_sem.at[which])


def place_kernel(*refs):
    sources, targets, held, in_sems, out_sems = refs[:4], refs[4:8], refs[8], refs[9], refs[10]
    rows = 32
    pieces = sources[0].shape[0] // rows

    def copies_of(which, piece):
        at = pl.ds(piece * rows, rows)
        index = which * pieces + piece
        return (
            pltpu.make_async_copy(
                sources[which].at[at, :], held.at[which, at, :], in_sems.at[index]
            ),
            pltpu.make_async_copy(
                held.at[which, at, :], targets[which].at[at, :], out_sems.at[index]
            ),
        )

    pairs = [copies_of(which, piece) for which in range(4) for piece in range(pieces)]
    for inward, _ in pairs:
        inward.start()
    for inward, outward in pairs:
        inward.wait()
        outward.start()
    for _, outward in pairs:
        outward.wait()


def place_outputs(results):
    hbm = pl.BlockSpec(memory_space=pltpu.HBM)
    pieces = 4 * (results[0].shape[0] // 32)
    return pl.pallas_call(
        place_kernel,
        out_shape=[jax.ShapeDtypeStruct(result.shape, BF16) for result in results],
        in_specs=[hbm] * 4,
        out_specs=[hbm] * 4,
        scratch_shapes=[
            pltpu.VMEM((4,) + results[0].shape, BF16),
            pltpu.SemaphoreType.DMA((pieces,)),
            pltpu.SemaphoreType.DMA((pieces,)),
        ],
        compiler_params=pltpu.CompilerParams(vmem_limit_bytes=VMEM_GRANT),
        name="place_outputs",
    )(*results)


def fused(
    n_dp,
    n_sp,
    queries,
    key_rows,
    value_rows,
    cotangent,
    lengths,
    sample_plan,
    guide_bins,
    guide_table,
    block_source,
):
    tok, row_width = queries.shape
    n = n_dp * n_sp
    heads_dev = HEADS // n_sp
    group_tok = tok * n_sp
    smem = pl.BlockSpec(memory_space=pltpu.SMEM)
    vmem = pl.BlockSpec(memory_space=pltpu.VMEM)
    hbm = pl.BlockSpec(memory_space=pltpu.HBM)
    flops = 2 * 8 * heads_dev * group_tok * group_tok * HD
    return pl.pallas_call(
        functools.partial(fused_kernel, n_dp, n_sp, tok // n, heads_dev),
        out_shape=[jax.ShapeDtypeStruct((tok, row_width), BF16)] * 4,
        in_specs=[smem] * 4 + [vmem] + [hbm] * 4,
        out_specs=[hbm] * 4,
        scratch_shapes=[
            pltpu.VMEM((heads_dev, n_sp, 3, tok, HD), BF16),
            pltpu.VMEM((HEADS, n_dp, 3, tok // n_dp, HD), BF16),
            pltpu.VMEM((heads_dev, n, 3, group_tok // n, HD), BF16),
            pltpu.VMEM((group_tok, heads_dev * HD), BF16),
            pltpu.VMEM((heads_dev, n, 3, group_tok // n, HD), BF16),
            pltpu.VMEM((HEADS, n_dp, 3, tok // n_dp, HD), BF16),
            pltpu.VMEM((heads_dev, group_tok, HD), BF16),
            pltpu.VMEM((HEADS, tok, HD), BF16),
            pltpu.VMEM((group_tok, group_tok), BF16),
            pltpu.VMEM((group_tok, group_tok), BF16),
            pltpu.VMEM((tok, tok), BF16),
            pltpu.VMEM((HEADS, 3, tok, HD), BF16),
            pltpu.SemaphoreType.DMA((heads_dev,)),
            pltpu.SemaphoreType.DMA((heads_dev,)),
            pltpu.SemaphoreType.DMA((heads_dev,)),
            pltpu.SemaphoreType.DMA((heads_dev,)),
            pltpu.SemaphoreType.DMA((heads_dev,)),
            pltpu.SemaphoreType.DMA,
            pltpu.SemaphoreType.DMA,
            pltpu.SemaphoreType.DMA((heads_dev,)),
            pltpu.SemaphoreType.DMA((heads_dev,)),
            pltpu.SemaphoreType.DMA((3 * heads_dev + 1,)),
            pltpu.SemaphoreType.DMA((4,)),
        ],
        compiler_params=pltpu.CompilerParams(
            collective_id=0, has_side_effects=True, vmem_limit_bytes=VMEM_GRANT
        ),
        cost_estimate=pl.CostEstimate(
            flops=flops, bytes_accessed=16 * tok * row_width, transcendentals=0
        ),
        name="routed_attention",
    )(
        lengths,
        sample_plan,
        guide_bins,
        guide_table,
        block_source.reshape(n_dp, block_source.shape[0] // n_dp),
        queries,
        key_rows,
        value_rows,
        cotangent,
    )


def chosen(*arrays):
    n_dp, n_sp = lax.axis_size("dp"), lax.axis_size("sp")
    tok = arrays[0].shape[0]
    block_rows = tok // (n_dp * n_sp)
    if (n_sp * block_rows) % 16 == 0 and HEADS % n_sp == 0:
        return place_outputs(fused(n_dp, n_sp, *arrays))
    return per_device(*arrays)


def solution(mesh):
    placed = (
        P(("dp", "sp"), None),
        P(("dp", "sp"), None),
        P(("dp", "sp"), None),
        P(("dp", "sp"), None),
        P(),
        P(),
        P(),
        P(),
        P(),
    )
    return jax.shard_map(
        chosen,
        mesh=mesh,
        in_specs=placed,
        out_specs=(
            P(("dp", "sp"), None),
            P(("dp", "sp"), None),
            P(("dp", "sp"), None),
            P(("dp", "sp"), None),
        ),
        check_vma=False,
    )
```

```python
import functools

import jax
import jax.numpy as jnp
from jax import lax
from jax.experimental import pallas as pl
from jax.experimental.pallas import tpu as pltpu
from jax.sharding import PartitionSpec as P

HEADS = 20
HD = 128
MESH = pl.DeviceIdType.MESH
VMEM_GRANT = 48 * 1024 * 1024
F32 = jnp.float32
BF16 = jnp.bfloat16


def head_pass(query_head, key_head, value_head, grad_head, query_live, key_live):
    scores = jnp.dot(query_head, key_head.T, preferred_element_type=jnp.float32) * HD ** (-0.5)
    masked = jnp.where(key_live[None, :], scores, -1e30)
    top_score = jnp.max(masked, axis=1, keepdims=True)
    shifted_exp = jnp.where(key_live[None, :], jnp.exp(masked - top_score), 0.0)
    row_total = jnp.sum(shifted_exp, axis=1, keepdims=True)
    attend = jnp.where(query_live[:, None], shifted_exp / row_total, 0.0)
    attend_bf = attend.astype(jnp.bfloat16)
    output = jnp.dot(attend_bf, value_head, preferred_element_type=jnp.float32)
    grad_attend = jnp.dot(grad_head, value_head.T, preferred_element_type=jnp.float32)
    row_dot = jnp.sum(grad_head.astype(jnp.float32) * output, axis=1, keepdims=True)
    grad_scores = (attend * (grad_attend - row_dot) * HD ** (-0.5)).astype(jnp.bfloat16)
    grad_query = jnp.dot(grad_scores, key_head, preferred_element_type=jnp.float32)
    grad_key = jnp.dot(grad_scores.T, query_head, preferred_element_type=jnp.float32)
    grad_value = jnp.dot(attend_bf.T, grad_head, preferred_element_type=jnp.float32)
    return (output, grad_query, grad_key, grad_value)


def head_stack(query_part, key_part, value_part, grad_part, query_live, key_live):

    def one_head(head_items):
        return head_pass(
            head_items[0], head_items[1], head_items[2], head_items[3], query_live, key_live
        )

    stacked = tuple(
        (jnp.moveaxis(source, 1, 0) for source in (query_part, key_part, value_part, grad_part))
    )
    return lax.map(one_head, stacked)


def dispatch(first, second, third):
    return (
        lax.all_to_all(first, ("dp", "sp"), split_axis=0, concat_axis=0, tiled=True),
        lax.all_to_all(second, ("dp", "sp"), split_axis=0, concat_axis=0, tiled=True),
        lax.all_to_all(third, ("dp", "sp"), split_axis=0, concat_axis=0, tiled=True),
    )


def send_back(first, second, third):
    return (
        lax.all_to_all(first, ("dp", "sp"), split_axis=0, concat_axis=0, tiled=True),
        lax.all_to_all(second, ("dp", "sp"), split_axis=0, concat_axis=0, tiled=True),
        lax.all_to_all(third, ("dp", "sp"), split_axis=0, concat_axis=0, tiled=True),
    )


def per_device(
    queries,
    key_rows,
    value_rows,
    cotangent,
    lengths,
    sample_plan,
    guide_bins,
    guide_table,
    block_source,
):
    n_dp = lax.axis_size("dp")
    n_sp = lax.axis_size("sp")
    loaders = n_dp * n_sp
    tok_rows = queries.shape[0]
    row_width = queries.shape[1]
    block_rows = tok_rows // loaders
    device_index = lax.axis_index("dp") * n_sp + lax.axis_index("sp")
    table = block_source.reshape(loaders, loaders)
    sources = table[device_index] // loaders
    send_slot = jnp.sum(jnp.where(table // loaders == device_index, table % loaders, 0), axis=1)
    slot_index = jnp.arange(loaders, dtype=jnp.int32)
    back_slot = jnp.sum(
        jnp.where(sources[None, :] == slot_index[:, None], slot_index[None, :], 0), axis=1
    )
    loader_slot = jnp.sum(
        jnp.where(send_slot[None, :] == slot_index[:, None], slot_index[None, :], 0), axis=1
    )

    def as_blocks(source, order):
        return source.reshape(loaders, block_rows, row_width)[order]

    recv_query, recv_key, recv_value = dispatch(
        as_blocks(queries, send_slot),
        as_blocks(key_rows, send_slot),
        as_blocks(value_rows, send_slot),
    )
    query_own = recv_query[sources].reshape(tok_rows, HEADS, HD)
    key_own = recv_key[sources].reshape(tok_rows, HEADS, HD)
    value_own = recv_value[sources].reshape(tok_rows, HEADS, HD)
    group_index = lax.axis_index("dp")
    picked = sample_plan == group_index
    group_len = jnp.sum(jnp.where(picked, lengths, 0))
    group_bin = jnp.sum(jnp.where(picked, guide_bins, 0))
    bin_match = jnp.arange(guide_table.shape[0], dtype=jnp.int32) == group_bin
    head_gate = jnp.sum(jnp.where(bin_match[:, None], guide_table, 0.0), axis=0)
    grad_own = (
        head_gate[None, :, None] * cotangent.reshape(tok_rows, HEADS, HD).astype(jnp.float32)
    ).astype(jnp.bfloat16)
    heads_dev = HEADS // n_sp
    split_shape = (tok_rows, n_sp, heads_dev, HD)
    group_items = (
        lax.all_to_all(
            query_own.reshape(split_shape), "sp", split_axis=1, concat_axis=0, tiled=True
        ),
        lax.all_to_all(key_own.reshape(split_shape), "sp", split_axis=1, concat_axis=0, tiled=True),
        lax.all_to_all(
            value_own.reshape(split_shape), "sp", split_axis=1, concat_axis=0, tiled=True
        ),
        lax.all_to_all(
            grad_own.reshape(split_shape), "sp", split_axis=1, concat_axis=0, tiled=True
        ),
    )
    flat_items = tuple((item[:, 0] for item in group_items))
    live_rows = jnp.arange(flat_items[0].shape[0], dtype=jnp.int32) < group_len
    results = head_stack(
        flat_items[0], flat_items[1], flat_items[2], flat_items[3], live_rows, live_rows
    )
    out_heads, gq_heads, gk_heads, gv_heads = tuple(
        (jnp.moveaxis(result, 0, 1)[:, None].astype(jnp.bfloat16) for result in results)
    )
    back_rows = (
        lax.all_to_all(out_heads, "sp", split_axis=0, concat_axis=1, tiled=True),
        lax.all_to_all(gq_heads, "sp", split_axis=0, concat_axis=1, tiled=True),
        lax.all_to_all(gk_heads, "sp", split_axis=0, concat_axis=1, tiled=True),
        lax.all_to_all(gv_heads, "sp", split_axis=0, concat_axis=1, tiled=True),
    )
    out_bf, grad_q_own, grad_k_own, grad_v_own = tuple(
        (part.reshape(tok_rows, HEADS, HD) for part in back_rows)
    )
    attn_out = (
        (head_gate[None, :, None] * lax.optimization_barrier(out_bf).astype(jnp.float32))
        .astype(jnp.bfloat16)
        .reshape(tok_rows, row_width)
    )
    back_query, back_key, back_value = send_back(
        as_blocks(grad_q_own, back_slot),
        as_blocks(grad_k_own, back_slot),
        as_blocks(grad_v_own, back_slot),
    )
    grad_queries = back_query[loader_slot].reshape(tok_rows, row_width)
    grad_keys = back_key[loader_slot].reshape(tok_rows, row_width)
    grad_values = back_value[loader_slot].reshape(tok_rows, row_width)
    return (attn_out, grad_queries, grad_keys, grad_values)


def dot_nn(left, right):
    return lax.dot_general(left, right, (((1,), (0,)), ((), ())), preferred_element_type=F32)


def dot_nt(left, right):
    return lax.dot_general(left, right, (((1,), (1,)), ((), ())), preferred_element_type=F32)


def dot_tn(left, right):
    return lax.dot_general(left, right, (((0,), (0,)), ((), ())), preferred_element_type=F32)


def iota(shape, axis):
    return lax.broadcasted_iota(jnp.int32, shape, axis)


def fused_kernel(
    n_dp,
    n_sp,
    block_rows,
    heads_dev,
    length_ref,
    plan_ref,
    bin_ref,
    table_ref,
    source_ref,
    q_ref,
    k_ref,
    v_ref,
    cot_ref,
    out_ref,
    gq_ref,
    gk_ref,
    gv_ref,
    load_buf,
    send_buf,
    recv_buf,
    cot_buf,
    grad_buf,
    back_buf,
    out_buf,
    oback_buf,
    order_buf,
    unorder_buf,
    pick_buf,
    load_sem,
    send_sem,
    recv_sem,
    gsend_sem,
    back_sem,
    csend_sem,
    crecv_sem,
    osend_sem,
    orecv_sem,
    local_sem,
):
    n = n_dp * n_sp
    chunk = n_sp * block_rows
    tok = q_ref.shape[0]
    group_tok = tok * n_sp
    group_blocks = group_tok // block_rows
    group = lax.axis_index("dp")
    part = lax.axis_index("sp")
    me = group * n_sp + part
    my_part_rows = pl.ds(pl.multiple_of(part * tok, tok), tok)

    batches = [
        (at, first, min(2, heads_dev - first)) for at, first in enumerate(range(0, heads_dev, 2))
    ]

    def load(j, carry):
        for part_to in range(n_sp):
            columns = pl.ds(pl.multiple_of((part_to * heads_dev + j) * HD, HD), HD)
            for which, ref in enumerate((q_ref, k_ref, v_ref)):
                pltpu.make_async_copy(
                    ref.at[:, columns], load_buf.at[j, part_to, which], load_sem.at[j]
                ).start()
        return carry

    barrier = pltpu.get_barrier_semaphore()
    load(0, 0)

    def greet(i, carry):
        peer = (me + 1 + i) % n
        pl.semaphore_signal(
            barrier, inc=1, device_id=(peer // n_sp, peer % n_sp), device_id_type=MESH
        )
        return carry

    lax.fori_loop(0, n - 1, greet, 0)
    lax.fori_loop(1, batches[0][2], load, 0)

    source = source_ref[...]
    loader_of = source // n
    mine = jnp.where(loader_of == me, source % n, 0)
    spread = jnp.broadcast_to(mine[:, None, :], (n_dp, chunk, group_blocks)).reshape(
        n_dp * chunk, group_blocks
    )
    row_part = (iota((n_dp * chunk, group_blocks), 0) // block_rows) % n_sp
    col_part = iota((n_dp * chunk, group_blocks), 1) // n
    slot = jnp.sum(jnp.where(row_part == col_part, spread, 0), axis=1, keepdims=True)
    pick_row = slot * block_rows + iota((n_dp * chunk, 1), 0) % block_rows
    pick_buf[...] = jnp.where(iota((n_dp * chunk, tok), 1) == pick_row, 1.0, 0.0).astype(BF16)

    def wait_bytes(ref, sem):
        pltpu.make_async_copy(ref, ref, sem).wait()

    def prepare(j):
        wait_bytes(load_buf.at[j], load_sem.at[j])
        for part_to in range(n_sp):
            head = part_to * heads_dev + j
            for which in range(3):
                send_buf[head, :, which] = (
                    dot_nn(pick_buf[...], load_buf[j, part_to, which])
                    .astype(BF16)
                    .reshape(n_dp, chunk, HD)
                )

    def peer_at(i):
        turn = i + (i + n - 3) // (n - 1)
        quarter = n // 4
        outer = (me // quarter + 6 - turn % 4) % 4
        peer = outer * quarter + (me % quarter + turn // 4) % quarter
        return peer // n_sp, peer % n_sp

    def forward(at, first, size):
        def one(i, carry):
            to_group, to_part = peer_at(i)
            pltpu.make_async_remote_copy(
                src_ref=send_buf.at[pl.ds(to_part * heads_dev + first, size), to_group],
                dst_ref=recv_buf.at[pl.ds(first, size), me],
                send_sem=send_sem.at[at],
                recv_sem=recv_sem.at[at],
                device_id=(to_group, to_part),
                device_id_type=MESH,
            ).start()
            return carry

        lax.fori_loop(0, n - 1, one, 0)
        pltpu.make_async_copy(
            send_buf.at[pl.ds(part * heads_dev + first, size), group],
            recv_buf.at[pl.ds(first, size), me],
            local_sem.at[at],
        ).start()

    def backward(at, first, size):
        def one(i, carry):
            to_group, to_part = peer_at(i)
            to = to_group * n_sp + to_part
            pltpu.make_async_remote_copy(
                src_ref=grad_buf.at[pl.ds(first, size), to],
                dst_ref=back_buf.at[pl.ds(part * heads_dev + first, size), group],
                send_sem=gsend_sem.at[at],
                recv_sem=back_sem.at[at],
                device_id=(to_group, to_part),
                device_id_type=MESH,
            ).start()
            return carry

        lax.fori_loop(0, n - 1, one, 0)
        pltpu.make_async_copy(
            grad_buf.at[pl.ds(first, size), me],
            back_buf.at[pl.ds(part * heads_dev + first, size), group],
            local_sem.at[heads_dev + at],
        ).start()

        for step in range(1, n_sp):
            to_part = (part + step) % n_sp
            pltpu.make_async_remote_copy(
                src_ref=out_buf.at[
                    pl.ds(first, size), pl.ds(pl.multiple_of(to_part * tok, tok), tok), :
                ],
                dst_ref=oback_buf.at[pl.ds(part * heads_dev + first, size)],
                send_sem=osend_sem.at[at],
                recv_sem=orecv_sem.at[at],
                device_id=(group, to_part),
                device_id_type=MESH,
            ).start()
        pltpu.make_async_copy(
            out_buf.at[pl.ds(first, size), my_part_rows, :],
            oback_buf.at[pl.ds(part * heads_dev + first, size)],
            local_sem.at[2 * heads_dev + at],
        ).start()

    width = heads_dev * HD
    def prepare_batch(first, size):
        def one(j, carry):
            prepare(j)
            return carry

        lax.fori_loop(first, first + size, one, 0)

    prepare_batch(0, batches[0][2])
    pl.semaphore_wait(barrier, n - 1)
    forward(*batches[0])
    lax.fori_loop(batches[0][2], heads_dev, load, 0)
    for step in range(1, n_sp):
        to_part = (part + step) % n_sp
        pltpu.make_async_remote_copy(
            src_ref=cot_ref.at[:, pl.ds(pl.multiple_of(to_part * width, HD), width)],
            dst_ref=cot_buf.at[my_part_rows, :],
            send_sem=csend_sem,
            recv_sem=crecv_sem,
            device_id=(group, to_part),
            device_id_type=MESH,
        ).start()
    pltpu.make_async_copy(
        cot_ref.at[:, pl.ds(pl.multiple_of(part * width, HD), width)],
        cot_buf.at[my_part_rows, :],
        local_sem.at[3 * heads_dev],
    ).start()

    for at, first, size in batches[1:]:
        prepare_batch(first, size)
        forward(at, first, size)

    group_len = jnp.int32(0)
    group_bin = jnp.int32(0)
    for sample in range(n_dp):
        picked = plan_ref[sample] == group
        group_len += jnp.where(picked, length_ref[sample], 0)
        group_bin += jnp.where(picked, bin_ref[sample], 0)

    loader_row = (source_ref[pl.ds(group, 1), :] // n).astype(F32)
    widen = jnp.where(
        iota((group_blocks, group_tok), 0) == iota((group_blocks, group_tok), 1) // block_rows,
        1.0,
        0.0,
    ).astype(BF16)
    place = iota((1, group_tok), 1)
    lane_loader = dot_nn(
        jnp.broadcast_to(loader_row, (16, group_blocks)).astype(BF16), widen
    )[0:1].astype(jnp.int32)
    lane_row = lane_loader * chunk + (place // tok) * block_rows + place % block_rows
    col_loader = jnp.sum(
        jnp.where(
            iota((group_tok, group_blocks), 1) == iota((group_tok, group_blocks), 0) // block_rows,
            loader_row,
            0.0,
        ),
        axis=1,
        keepdims=True,
    ).astype(jnp.int32)
    col_place = iota((group_tok, 1), 0)
    col_row = col_loader * chunk + (col_place // tok) * block_rows + col_place % block_rows
    square = (group_tok, group_tok)
    order = jnp.where(iota(square, 0) == lane_row, 1.0, 0.0)
    unorder = jnp.where(iota(square, 1) == col_row, 1.0, 0.0)
    order_buf[...] = order.astype(BF16)
    unorder_buf[...] = unorder.astype(BF16)
    key_live = jnp.sum(jnp.where(place < group_len, order, 0.0), axis=1, keepdims=True)
    query_live = jnp.sum(jnp.where(col_place < group_len, unorder, 0.0), axis=0, keepdims=True)

    wait_bytes(cot_buf.at[pl.ds(0, (n_sp - 1) * tok), :], crecv_sem)
    wait_bytes(cot_buf.at[my_part_rows, :], local_sem.at[3 * heads_dev])

    scale = HD ** (-0.5)

    def one_head(j, carry):
        gate = table_ref[group_bin, part * heads_dev + j]
        columns = pl.ds(pl.multiple_of(j * HD, HD), HD)
        d_out = (gate * dot_nn(order_buf[...], cot_buf[:, columns])).astype(BF16)
        for at, first, size in batches:

            @pl.when(j == first)
            def _():
                heads = pl.ds(first, size)
                wait_bytes(recv_buf.at[heads, pl.ds(0, n - 1)], recv_sem.at[at])
                wait_bytes(recv_buf.at[heads, me], local_sem.at[at])

        query, key, value = (recv_buf[j, :, at].reshape(group_tok, HD) for at in range(3))
        scores = dot_nt(key, query) * scale
        scores = jnp.where(key_live > 0.5, scores, -1e30)
        top = jnp.max(scores, axis=0, keepdims=True)
        shifted = jnp.exp(scores - top)
        total = jnp.sum(shifted, axis=0, keepdims=True)
        attend = shifted * (query_live / total)
        attend_bf = attend.astype(BF16)
        grad_attend = dot_nt(value, d_out)
        row_dot = jnp.sum(attend_bf.astype(F32) * grad_attend, axis=0, keepdims=True)
        grad_scores = (attend * (grad_attend - row_dot) * scale).astype(BF16)
        grad_buf[j, :, 2] = dot_nn(attend_bf, d_out).astype(BF16).reshape(n, chunk, HD)
        grad_buf[j, :, 1] = dot_nn(grad_scores, query).astype(BF16).reshape(n, chunk, HD)
        grad_buf[j, :, 0] = dot_tn(grad_scores, key).astype(BF16).reshape(n, chunk, HD)
        output = dot_tn(attend_bf, value).astype(BF16)
        gated = (gate * output.astype(F32)).astype(BF16)
        out_buf[j] = dot_nn(unorder_buf[...], gated).astype(BF16)
        for at, first, size in batches:

            @pl.when(j == first + size - 1)
            def _():
                backward(at, first, size)

        return carry

    lax.fori_loop(0, heads_dev, one_head, 0)

    def collect(j, carry):
        for at, first, size in batches:

            @pl.when(j == first)
            def _():
                heads = pl.ds(first, size)
                wait_bytes(recv_buf.at[heads, pl.ds(0, n - 1)], back_sem.at[at])
                wait_bytes(recv_buf.at[heads, me], local_sem.at[heads_dev + at])
                wait_bytes(out_buf.at[heads, pl.ds(0, (n_sp - 1) * tok), :], orecv_sem.at[at])
                wait_bytes(out_buf.at[heads, my_part_rows, :], local_sem.at[2 * heads_dev + at])

        for part_from in range(n_sp):
            head = part_from * heads_dev + j
            columns = pl.ds(pl.multiple_of(head * HD, HD), HD)
            out_ref[:, columns] = oback_buf[head]
            for which, ref in enumerate((gq_ref, gk_ref, gv_ref)):
                arrived = back_buf[head, :, which].reshape(n_dp * chunk, HD)
                ref[:, columns] = dot_tn(pick_buf[...], arrived).astype(BF16)
        return carry

    lax.fori_loop(0, heads_dev, collect, 0)

    for at, first, size in batches:
        heads = pl.ds(first, size)
        wait_bytes(recv_buf.at[heads, pl.ds(0, n - 1)], send_sem.at[at])
        wait_bytes(recv_buf.at[heads, pl.ds(0, n - 1)], gsend_sem.at[at])
        wait_bytes(out_buf.at[heads, pl.ds(0, (n_sp - 1) * tok), :], osend_sem.at[at])
    wait_bytes(cot_buf.at[pl.ds(0, (n_sp - 1) * tok), :], csend_sem)


def place_kernel(*refs):
    sources, targets, sems = refs[:4], refs[4:8], refs[8]
    rows = 32
    pieces = sources[0].shape[0] // rows
    copies = []
    for which in range(4):
        for piece in range(pieces):
            at = pl.ds(piece * rows, rows)
            copies.append(
                pltpu.make_async_copy(
                    sources[which].at[at, :], targets[which].at[at, :], sems.at[len(copies)]
                )
            )
            copies[-1].start()
    for copy in copies:
        copy.wait()


def place_outputs(results):
    return pl.pallas_call(
        place_kernel,
        out_shape=[jax.ShapeDtypeStruct(result.shape, BF16) for result in results],
        in_specs=[pl.BlockSpec(memory_space=pltpu.VMEM)] * 4,
        out_specs=[pl.BlockSpec(memory_space=pltpu.HBM)] * 4,
        scratch_shapes=[pltpu.SemaphoreType.DMA((4 * (results[0].shape[0] // 32),))],
        compiler_params=pltpu.CompilerParams(vmem_limit_bytes=16 * 1024 * 1024),
        name="place_outputs",
    )(*results)


def fused(
    n_dp,
    n_sp,
    queries,
    key_rows,
    value_rows,
    cotangent,
    lengths,
    sample_plan,
    guide_bins,
    guide_table,
    block_source,
):
    tok, row_width = queries.shape
    n = n_dp * n_sp
    heads_dev = HEADS // n_sp
    group_tok = tok * n_sp
    smem = pl.BlockSpec(memory_space=pltpu.SMEM)
    vmem = pl.BlockSpec(memory_space=pltpu.VMEM)
    hbm = pl.BlockSpec(memory_space=pltpu.HBM)
    flops = 2 * 8 * heads_dev * group_tok * group_tok * HD
    return pl.pallas_call(
        functools.partial(fused_kernel, n_dp, n_sp, tok // n, heads_dev),
        out_shape=[jax.ShapeDtypeStruct((tok, row_width), BF16)] * 4,
        in_specs=[smem] * 4 + [vmem] + [hbm] * 4,
        out_specs=[vmem] * 4,
        scratch_shapes=[
            pltpu.VMEM((heads_dev, n_sp, 3, tok, HD), BF16),
            pltpu.VMEM((HEADS, n_dp, 3, tok // n_dp, HD), BF16),
            pltpu.VMEM((heads_dev, n, 3, group_tok // n, HD), BF16),
            pltpu.VMEM((group_tok, heads_dev * HD), BF16),
            pltpu.VMEM((heads_dev, n, 3, group_tok // n, HD), BF16),
            pltpu.VMEM((HEADS, n_dp, 3, tok // n_dp, HD), BF16),
            pltpu.VMEM((heads_dev, group_tok, HD), BF16),
            pltpu.VMEM((HEADS, tok, HD), BF16),
            pltpu.VMEM((group_tok, group_tok), BF16),
            pltpu.VMEM((group_tok, group_tok), BF16),
            pltpu.VMEM((tok, tok), BF16),
            pltpu.SemaphoreType.DMA((heads_dev,)),
            pltpu.SemaphoreType.DMA((heads_dev,)),
            pltpu.SemaphoreType.DMA((heads_dev,)),
            pltpu.SemaphoreType.DMA((heads_dev,)),
            pltpu.SemaphoreType.DMA((heads_dev,)),
            pltpu.SemaphoreType.DMA,
            pltpu.SemaphoreType.DMA,
            pltpu.SemaphoreType.DMA((heads_dev,)),
            pltpu.SemaphoreType.DMA((heads_dev,)),
            pltpu.SemaphoreType.DMA((3 * heads_dev + 1,)),
        ],
        compiler_params=pltpu.CompilerParams(
            collective_id=0, has_side_effects=True, vmem_limit_bytes=VMEM_GRANT
        ),
        cost_estimate=pl.CostEstimate(
            flops=flops, bytes_accessed=16 * tok * row_width, transcendentals=0
        ),
        name="routed_attention",
    )(
        *(
            pltpu.with_memory_space_constraint(array, pltpu.HBM)
            for array in (
                lengths,
                sample_plan,
                guide_bins,
                guide_table,
                block_source.reshape(n_dp, block_source.shape[0] // n_dp),
                queries,
                key_rows,
                value_rows,
                cotangent,
            )
        ),
    )


def chosen(*arrays):
    n_dp, n_sp = lax.axis_size("dp"), lax.axis_size("sp")
    tok = arrays[0].shape[0]
    block_rows = tok // (n_dp * n_sp)
    if (n_sp * block_rows) % 16 == 0 and HEADS % n_sp == 0:
        return place_outputs(fused(n_dp, n_sp, *arrays))
    return per_device(*arrays)


def solution(mesh):
    placed = (
        P(("dp", "sp"), None),
        P(("dp", "sp"), None),
        P(("dp", "sp"), None),
        P(("dp", "sp"), None),
        P(),
        P(),
        P(),
        P(),
        P(),
    )
    return jax.shard_map(
        chosen,
        mesh=mesh,
        in_specs=placed,
        out_specs=(
            P(("dp", "sp"), None),
            P(("dp", "sp"), None),
            P(("dp", "sp"), None),
            P(("dp", "sp"), None),
        ),
        check_vma=False,
    )
```

```python
import functools

import jax
import jax.numpy as jnp
from jax import lax
from jax.experimental import pallas as pl
from jax.experimental.pallas import tpu as pltpu
from jax.sharding import PartitionSpec as P

HEADS = 20
HD = 128
MESH = pl.DeviceIdType.MESH
VMEM_GRANT = 48 * 1024 * 1024
F32 = jnp.float32
BF16 = jnp.bfloat16


def head_pass(query_head, key_head, value_head, grad_head, query_live, key_live):
    scores = jnp.dot(query_head, key_head.T, preferred_element_type=jnp.float32) * HD ** (-0.5)
    masked = jnp.where(key_live[None, :], scores, -1e30)
    top_score = jnp.max(masked, axis=1, keepdims=True)
    shifted_exp = jnp.where(key_live[None, :], jnp.exp(masked - top_score), 0.0)
    row_total = jnp.sum(shifted_exp, axis=1, keepdims=True)
    attend = jnp.where(query_live[:, None], shifted_exp / row_total, 0.0)
    attend_bf = attend.astype(jnp.bfloat16)
    output = jnp.dot(attend_bf, value_head, preferred_element_type=jnp.float32)
    grad_attend = jnp.dot(grad_head, value_head.T, preferred_element_type=jnp.float32)
    row_dot = jnp.sum(grad_head.astype(jnp.float32) * output, axis=1, keepdims=True)
    grad_scores = (attend * (grad_attend - row_dot) * HD ** (-0.5)).astype(jnp.bfloat16)
    grad_query = jnp.dot(grad_scores, key_head, preferred_element_type=jnp.float32)
    grad_key = jnp.dot(grad_scores.T, query_head, preferred_element_type=jnp.float32)
    grad_value = jnp.dot(attend_bf.T, grad_head, preferred_element_type=jnp.float32)
    return (output, grad_query, grad_key, grad_value)


def head_stack(query_part, key_part, value_part, grad_part, query_live, key_live):

    def one_head(head_items):
        return head_pass(
            head_items[0], head_items[1], head_items[2], head_items[3], query_live, key_live
        )

    stacked = tuple(
        (jnp.moveaxis(source, 1, 0) for source in (query_part, key_part, value_part, grad_part))
    )
    return lax.map(one_head, stacked)


def dispatch(first, second, third):
    return (
        lax.all_to_all(first, ("dp", "sp"), split_axis=0, concat_axis=0, tiled=True),
        lax.all_to_all(second, ("dp", "sp"), split_axis=0, concat_axis=0, tiled=True),
        lax.all_to_all(third, ("dp", "sp"), split_axis=0, concat_axis=0, tiled=True),
    )


def send_back(first, second, third):
    return (
        lax.all_to_all(first, ("dp", "sp"), split_axis=0, concat_axis=0, tiled=True),
        lax.all_to_all(second, ("dp", "sp"), split_axis=0, concat_axis=0, tiled=True),
        lax.all_to_all(third, ("dp", "sp"), split_axis=0, concat_axis=0, tiled=True),
    )


def per_device(
    queries,
    key_rows,
    value_rows,
    cotangent,
    lengths,
    sample_plan,
    guide_bins,
    guide_table,
    block_source,
):
    n_dp = lax.axis_size("dp")
    n_sp = lax.axis_size("sp")
    loaders = n_dp * n_sp
    tok_rows = queries.shape[0]
    row_width = queries.shape[1]
    block_rows = tok_rows // loaders
    device_index = lax.axis_index("dp") * n_sp + lax.axis_index("sp")
    table = block_source.reshape(loaders, loaders)
    sources = table[device_index] // loaders
    send_slot = jnp.sum(jnp.where(table // loaders == device_index, table % loaders, 0), axis=1)
    slot_index = jnp.arange(loaders, dtype=jnp.int32)
    back_slot = jnp.sum(
        jnp.where(sources[None, :] == slot_index[:, None], slot_index[None, :], 0), axis=1
    )
    loader_slot = jnp.sum(
        jnp.where(send_slot[None, :] == slot_index[:, None], slot_index[None, :], 0), axis=1
    )

    def as_blocks(source, order):
        return source.reshape(loaders, block_rows, row_width)[order]

    recv_query, recv_key, recv_value = dispatch(
        as_blocks(queries, send_slot),
        as_blocks(key_rows, send_slot),
        as_blocks(value_rows, send_slot),
    )
    query_own = recv_query[sources].reshape(tok_rows, HEADS, HD)
    key_own = recv_key[sources].reshape(tok_rows, HEADS, HD)
    value_own = recv_value[sources].reshape(tok_rows, HEADS, HD)
    group_index = lax.axis_index("dp")
    picked = sample_plan == group_index
    group_len = jnp.sum(jnp.where(picked, lengths, 0))
    group_bin = jnp.sum(jnp.where(picked, guide_bins, 0))
    bin_match = jnp.arange(guide_table.shape[0], dtype=jnp.int32) == group_bin
    head_gate = jnp.sum(jnp.where(bin_match[:, None], guide_table, 0.0), axis=0)
    grad_own = (
        head_gate[None, :, None] * cotangent.reshape(tok_rows, HEADS, HD).astype(jnp.float32)
    ).astype(jnp.bfloat16)
    heads_dev = HEADS // n_sp
    split_shape = (tok_rows, n_sp, heads_dev, HD)
    group_items = (
        lax.all_to_all(
            query_own.reshape(split_shape), "sp", split_axis=1, concat_axis=0, tiled=True
        ),
        lax.all_to_all(key_own.reshape(split_shape), "sp", split_axis=1, concat_axis=0, tiled=True),
        lax.all_to_all(
            value_own.reshape(split_shape), "sp", split_axis=1, concat_axis=0, tiled=True
        ),
        lax.all_to_all(
            grad_own.reshape(split_shape), "sp", split_axis=1, concat_axis=0, tiled=True
        ),
    )
    flat_items = tuple((item[:, 0] for item in group_items))
    live_rows = jnp.arange(flat_items[0].shape[0], dtype=jnp.int32) < group_len
    results = head_stack(
        flat_items[0], flat_items[1], flat_items[2], flat_items[3], live_rows, live_rows
    )
    out_heads, gq_heads, gk_heads, gv_heads = tuple(
        (jnp.moveaxis(result, 0, 1)[:, None].astype(jnp.bfloat16) for result in results)
    )
    back_rows = (
        lax.all_to_all(out_heads, "sp", split_axis=0, concat_axis=1, tiled=True),
        lax.all_to_all(gq_heads, "sp", split_axis=0, concat_axis=1, tiled=True),
        lax.all_to_all(gk_heads, "sp", split_axis=0, concat_axis=1, tiled=True),
        lax.all_to_all(gv_heads, "sp", split_axis=0, concat_axis=1, tiled=True),
    )
    out_bf, grad_q_own, grad_k_own, grad_v_own = tuple(
        (part.reshape(tok_rows, HEADS, HD) for part in back_rows)
    )
    attn_out = (
        (head_gate[None, :, None] * lax.optimization_barrier(out_bf).astype(jnp.float32))
        .astype(jnp.bfloat16)
        .reshape(tok_rows, row_width)
    )
    back_query, back_key, back_value = send_back(
        as_blocks(grad_q_own, back_slot),
        as_blocks(grad_k_own, back_slot),
        as_blocks(grad_v_own, back_slot),
    )
    grad_queries = back_query[loader_slot].reshape(tok_rows, row_width)
    grad_keys = back_key[loader_slot].reshape(tok_rows, row_width)
    grad_values = back_value[loader_slot].reshape(tok_rows, row_width)
    return (attn_out, grad_queries, grad_keys, grad_values)


def dot_nn(left, right):
    return lax.dot_general(left, right, (((1,), (0,)), ((), ())), preferred_element_type=F32)


def dot_nt(left, right):
    return lax.dot_general(left, right, (((1,), (1,)), ((), ())), preferred_element_type=F32)


def dot_tn(left, right):
    return lax.dot_general(left, right, (((0,), (0,)), ((), ())), preferred_element_type=F32)


def iota(shape, axis):
    return lax.broadcasted_iota(jnp.int32, shape, axis)


def fused_kernel(
    n_dp,
    n_sp,
    block_rows,
    heads_dev,
    length_ref,
    plan_ref,
    bin_ref,
    table_ref,
    source_ref,
    q_ref,
    k_ref,
    v_ref,
    cot_ref,
    out_ref,
    gq_ref,
    gk_ref,
    gv_ref,
    load_buf,
    send_buf,
    recv_buf,
    cot_buf,
    grad_buf,
    back_buf,
    out_buf,
    oback_buf,
    order_buf,
    unorder_buf,
    pick_buf,
    load_sem,
    send_sem,
    recv_sem,
    gsend_sem,
    back_sem,
    csend_sem,
    crecv_sem,
    osend_sem,
    orecv_sem,
    local_sem,
):
    n = n_dp * n_sp
    chunk = n_sp * block_rows
    tok = q_ref.shape[0]
    group_tok = tok * n_sp
    group_blocks = group_tok // block_rows
    group = lax.axis_index("dp")
    part = lax.axis_index("sp")
    me = group * n_sp + part
    my_part_rows = pl.ds(pl.multiple_of(part * tok, tok), tok)

    starts = [0] + list(range(1, heads_dev - 2, 2)) + [heads_dev - 2, heads_dev - 1]
    batches = [
        (at, first, last - first)
        for at, (first, last) in enumerate(zip(starts, starts[1:] + [heads_dev]))
    ]

    def load(j, carry):
        for part_to in range(n_sp):
            columns = pl.ds(pl.multiple_of((part_to * heads_dev + j) * HD, HD), HD)
            for which, ref in enumerate((q_ref, k_ref, v_ref)):
                pltpu.make_async_copy(
                    ref.at[:, columns], load_buf.at[j, part_to, which], load_sem.at[j]
                ).start()
        return carry

    barrier = pltpu.get_barrier_semaphore()

    def greet(i, carry):
        peer = (me + 1 + i) % n
        pl.semaphore_signal(
            barrier, inc=1, device_id=(peer // n_sp, peer % n_sp), device_id_type=MESH
        )
        return carry

    lax.fori_loop(0, n - 1, greet, 0)
    load(0, 0)

    source = source_ref[...]
    loader_of = source // n
    mine = jnp.where(loader_of == me, source % n, 0)
    spread = jnp.broadcast_to(mine[:, None, :], (n_dp, chunk, group_blocks)).reshape(
        n_dp * chunk, group_blocks
    )
    row_part = (iota((n_dp * chunk, group_blocks), 0) // block_rows) % n_sp
    col_part = iota((n_dp * chunk, group_blocks), 1) // n
    slot = jnp.sum(jnp.where(row_part == col_part, spread, 0), axis=1, keepdims=True)
    pick_row = slot * block_rows + iota((n_dp * chunk, 1), 0) % block_rows
    pick_buf[...] = jnp.where(iota((n_dp * chunk, tok), 1) == pick_row, 1.0, 0.0).astype(BF16)

    def wait_bytes(ref, sem):
        pltpu.make_async_copy(ref, ref, sem).wait()

    def prepare(j):
        wait_bytes(load_buf.at[j], load_sem.at[j])
        for part_to in range(n_sp):
            head = part_to * heads_dev + j
            for which in range(3):
                send_buf[head, :, which] = (
                    dot_nn(pick_buf[...], load_buf[j, part_to, which])
                    .astype(BF16)
                    .reshape(n_dp, chunk, HD)
                )

    def peer_at(i):
        turn = i + (i + n - 3) // (n - 1)
        quarter = n // 4
        outer = (me // quarter + 6 - turn % 4) % 4
        peer = outer * quarter + (me % quarter + turn // 4) % quarter
        return peer // n_sp, peer % n_sp

    def forward(at, first, size):
        def one(i, carry):
            to_group, to_part = peer_at(i)
            pltpu.make_async_remote_copy(
                src_ref=send_buf.at[pl.ds(to_part * heads_dev + first, size), to_group],
                dst_ref=recv_buf.at[pl.ds(first, size), me],
                send_sem=send_sem.at[at],
                recv_sem=recv_sem.at[at],
                device_id=(to_group, to_part),
                device_id_type=MESH,
            ).start()
            return carry

        lax.fori_loop(0, n - 1, one, 0)
        pltpu.make_async_copy(
            send_buf.at[pl.ds(part * heads_dev + first, size), group],
            recv_buf.at[pl.ds(first, size), me],
            local_sem.at[at],
        ).start()

    def backward(at, first, size):
        def one(i, carry):
            to_group, to_part = peer_at(i)
            to = to_group * n_sp + to_part
            pltpu.make_async_remote_copy(
                src_ref=grad_buf.at[pl.ds(first, size), to],
                dst_ref=back_buf.at[pl.ds(part * heads_dev + first, size), group],
                send_sem=gsend_sem.at[at],
                recv_sem=back_sem.at[at],
                device_id=(to_group, to_part),
                device_id_type=MESH,
            ).start()
            return carry

        lax.fori_loop(0, n - 1, one, 0)
        pltpu.make_async_copy(
            grad_buf.at[pl.ds(first, size), me],
            back_buf.at[pl.ds(part * heads_dev + first, size), group],
            local_sem.at[heads_dev + at],
        ).start()

        for step in range(1, n_sp):
            to_part = (part + step) % n_sp
            pltpu.make_async_remote_copy(
                src_ref=out_buf.at[
                    pl.ds(first, size), pl.ds(pl.multiple_of(to_part * tok, tok), tok), :
                ],
                dst_ref=oback_buf.at[pl.ds(part * heads_dev + first, size)],
                send_sem=osend_sem.at[at],
                recv_sem=orecv_sem.at[at],
                device_id=(group, to_part),
                device_id_type=MESH,
            ).start()
        pltpu.make_async_copy(
            out_buf.at[pl.ds(first, size), my_part_rows, :],
            oback_buf.at[pl.ds(part * heads_dev + first, size)],
            local_sem.at[2 * heads_dev + at],
        ).start()

    width = heads_dev * HD
    def prepare_batch(first, size):
        def one(j, carry):
            prepare(j)
            return carry

        lax.fori_loop(first, first + size, one, 0)

    prepare_batch(0, batches[0][2])
    pl.semaphore_wait(barrier, n - 1)
    forward(*batches[0])
    lax.fori_loop(batches[0][2], heads_dev, load, 0)
    for step in range(1, n_sp):
        to_part = (part + step) % n_sp
        pltpu.make_async_remote_copy(
            src_ref=cot_ref.at[:, pl.ds(pl.multiple_of(to_part * width, HD), width)],
            dst_ref=cot_buf.at[my_part_rows, :],
            send_sem=csend_sem,
            recv_sem=crecv_sem,
            device_id=(group, to_part),
            device_id_type=MESH,
        ).start()
    pltpu.make_async_copy(
        cot_ref.at[:, pl.ds(pl.multiple_of(part * width, HD), width)],
        cot_buf.at[my_part_rows, :],
        local_sem.at[3 * heads_dev],
    ).start()

    for at, first, size in batches[1:]:
        prepare_batch(first, size)
        forward(at, first, size)

    group_len = jnp.int32(0)
    group_bin = jnp.int32(0)
    for sample in range(n_dp):
        picked = plan_ref[sample] == group
        group_len += jnp.where(picked, length_ref[sample], 0)
        group_bin += jnp.where(picked, bin_ref[sample], 0)

    loader_row = (source_ref[pl.ds(group, 1), :] // n).astype(F32)
    widen = jnp.where(
        iota((group_blocks, group_tok), 0) == iota((group_blocks, group_tok), 1) // block_rows,
        1.0,
        0.0,
    ).astype(BF16)
    place = iota((1, group_tok), 1)
    lane_loader = dot_nn(
        jnp.broadcast_to(loader_row, (16, group_blocks)).astype(BF16), widen
    )[0:1].astype(jnp.int32)
    lane_row = lane_loader * chunk + (place // tok) * block_rows + place % block_rows
    col_loader = jnp.sum(
        jnp.where(
            iota((group_tok, group_blocks), 1) == iota((group_tok, group_blocks), 0) // block_rows,
            loader_row,
            0.0,
        ),
        axis=1,
        keepdims=True,
    ).astype(jnp.int32)
    col_place = iota((group_tok, 1), 0)
    col_row = col_loader * chunk + (col_place // tok) * block_rows + col_place % block_rows
    square = (group_tok, group_tok)
    order = jnp.where(iota(square, 0) == lane_row, 1.0, 0.0)
    unorder = jnp.where(iota(square, 1) == col_row, 1.0, 0.0)
    order_buf[...] = order.astype(BF16)
    unorder_buf[...] = unorder.astype(BF16)
    key_live = jnp.sum(jnp.where(place < group_len, order, 0.0), axis=1, keepdims=True)
    query_live = jnp.sum(jnp.where(col_place < group_len, unorder, 0.0), axis=0, keepdims=True)

    wait_bytes(cot_buf.at[pl.ds(0, (n_sp - 1) * tok), :], crecv_sem)
    wait_bytes(cot_buf.at[my_part_rows, :], local_sem.at[3 * heads_dev])

    scale = HD ** (-0.5)

    def one_head(j, carry):
        gate = table_ref[group_bin, part * heads_dev + j]
        columns = pl.ds(pl.multiple_of(j * HD, HD), HD)
        d_out = (gate * dot_nn(order_buf[...], cot_buf[:, columns])).astype(BF16)
        for at, first, size in batches:

            @pl.when(j == first)
            def _():
                heads = pl.ds(first, size)
                wait_bytes(recv_buf.at[heads, pl.ds(0, n - 1)], recv_sem.at[at])
                wait_bytes(recv_buf.at[heads, me], local_sem.at[at])

        query, key, value = (recv_buf[j, :, at].reshape(group_tok, HD) for at in range(3))
        scores = dot_nt(key, query) * scale
        scores = jnp.where(key_live > 0.5, scores, -1e30)
        top = jnp.max(scores, axis=0, keepdims=True)
        shifted = jnp.exp(scores - top)
        total = jnp.sum(shifted, axis=0, keepdims=True)
        attend = shifted * (query_live / total)
        attend_bf = attend.astype(BF16)
        grad_attend = dot_nt(value, d_out)
        row_dot = jnp.sum(attend_bf.astype(F32) * grad_attend, axis=0, keepdims=True)
        grad_scores = (attend * (grad_attend - row_dot) * scale).astype(BF16)
        grad_buf[j, :, 2] = dot_nn(attend_bf, d_out).astype(BF16).reshape(n, chunk, HD)
        grad_buf[j, :, 1] = dot_nn(grad_scores, query).astype(BF16).reshape(n, chunk, HD)
        grad_buf[j, :, 0] = dot_tn(grad_scores, key).astype(BF16).reshape(n, chunk, HD)
        output = dot_tn(attend_bf, value).astype(BF16)
        gated = (gate * output.astype(F32)).astype(BF16)
        out_buf[j] = dot_nn(unorder_buf[...], gated).astype(BF16)
        for at, first, size in batches:

            @pl.when(j == first + size - 1)
            def _():
                backward(at, first, size)

        return carry

    lax.fori_loop(0, heads_dev, one_head, 0)

    def collect(j, carry):
        for at, first, size in batches:

            @pl.when(j == first)
            def _():
                heads = pl.ds(first, size)
                wait_bytes(recv_buf.at[heads, pl.ds(0, n - 1)], back_sem.at[at])
                wait_bytes(recv_buf.at[heads, me], local_sem.at[heads_dev + at])
                wait_bytes(out_buf.at[heads, pl.ds(0, (n_sp - 1) * tok), :], orecv_sem.at[at])
                wait_bytes(out_buf.at[heads, my_part_rows, :], local_sem.at[2 * heads_dev + at])

        for part_from in range(n_sp):
            head = part_from * heads_dev + j
            columns = pl.ds(pl.multiple_of(head * HD, HD), HD)
            out_ref[:, columns] = oback_buf[head]
            for which, ref in enumerate((gq_ref, gk_ref, gv_ref)):
                arrived = back_buf[head, :, which].reshape(n_dp * chunk, HD)
                ref[:, columns] = dot_tn(pick_buf[...], arrived).astype(BF16)
        return carry

    lax.fori_loop(0, heads_dev, collect, 0)

    for at, first, size in batches:
        heads = pl.ds(first, size)
        wait_bytes(recv_buf.at[heads, pl.ds(0, n - 1)], send_sem.at[at])
        wait_bytes(recv_buf.at[heads, pl.ds(0, n - 1)], gsend_sem.at[at])
        wait_bytes(out_buf.at[heads, pl.ds(0, (n_sp - 1) * tok), :], osend_sem.at[at])
    wait_bytes(cot_buf.at[pl.ds(0, (n_sp - 1) * tok), :], csend_sem)


def place_kernel(*refs):
    sources, targets, sems = refs[:4], refs[4:8], refs[8]
    rows = 32
    pieces = sources[0].shape[0] // rows
    copies = []
    for which in range(4):
        for piece in range(pieces):
            at = pl.ds(piece * rows, rows)
            copies.append(
                pltpu.make_async_copy(
                    sources[which].at[at, :], targets[which].at[at, :], sems.at[len(copies)]
                )
            )
            copies[-1].start()
    for copy in copies:
        copy.wait()


def place_outputs(results):
    return pl.pallas_call(
        place_kernel,
        out_shape=[jax.ShapeDtypeStruct(result.shape, BF16) for result in results],
        in_specs=[pl.BlockSpec(memory_space=pltpu.VMEM)] * 4,
        out_specs=[pl.BlockSpec(memory_space=pltpu.HBM)] * 4,
        scratch_shapes=[pltpu.SemaphoreType.DMA((4 * (results[0].shape[0] // 32),))],
        compiler_params=pltpu.CompilerParams(vmem_limit_bytes=16 * 1024 * 1024),
        name="place_outputs",
    )(*results)


def fused(
    n_dp,
    n_sp,
    queries,
    key_rows,
    value_rows,
    cotangent,
    lengths,
    sample_plan,
    guide_bins,
    guide_table,
    block_source,
):
    tok, row_width = queries.shape
    n = n_dp * n_sp
    heads_dev = HEADS // n_sp
    group_tok = tok * n_sp
    smem = pl.BlockSpec(memory_space=pltpu.SMEM)
    vmem = pl.BlockSpec(memory_space=pltpu.VMEM)
    hbm = pl.BlockSpec(memory_space=pltpu.HBM)
    flops = 2 * 8 * heads_dev * group_tok * group_tok * HD
    return pl.pallas_call(
        functools.partial(fused_kernel, n_dp, n_sp, tok // n, heads_dev),
        out_shape=[jax.ShapeDtypeStruct((tok, row_width), BF16)] * 4,
        in_specs=[smem] * 4 + [vmem] + [hbm] * 4,
        out_specs=[vmem] * 4,
        scratch_shapes=[
            pltpu.VMEM((heads_dev, n_sp, 3, tok, HD), BF16),
            pltpu.VMEM((HEADS, n_dp, 3, tok // n_dp, HD), BF16),
            pltpu.VMEM((heads_dev, n, 3, group_tok // n, HD), BF16),
            pltpu.VMEM((group_tok, heads_dev * HD), BF16),
            pltpu.VMEM((heads_dev, n, 3, group_tok // n, HD), BF16),
            pltpu.VMEM((HEADS, n_dp, 3, tok // n_dp, HD), BF16),
            pltpu.VMEM((heads_dev, group_tok, HD), BF16),
            pltpu.VMEM((HEADS, tok, HD), BF16),
            pltpu.VMEM((group_tok, group_tok), BF16),
            pltpu.VMEM((group_tok, group_tok), BF16),
            pltpu.VMEM((tok, tok), BF16),
            pltpu.SemaphoreType.DMA((heads_dev,)),
            pltpu.SemaphoreType.DMA((heads_dev,)),
            pltpu.SemaphoreType.DMA((heads_dev,)),
            pltpu.SemaphoreType.DMA((heads_dev,)),
            pltpu.SemaphoreType.DMA((heads_dev,)),
            pltpu.SemaphoreType.DMA,
            pltpu.SemaphoreType.DMA,
            pltpu.SemaphoreType.DMA((heads_dev,)),
            pltpu.SemaphoreType.DMA((heads_dev,)),
            pltpu.SemaphoreType.DMA((3 * heads_dev + 1,)),
        ],
        compiler_params=pltpu.CompilerParams(
            collective_id=0, has_side_effects=True, vmem_limit_bytes=VMEM_GRANT
        ),
        cost_estimate=pl.CostEstimate(
            flops=flops, bytes_accessed=16 * tok * row_width, transcendentals=0
        ),
        name="routed_attention",
    )(
        *(
            pltpu.with_memory_space_constraint(array, pltpu.HBM)
            for array in (
                lengths,
                sample_plan,
                guide_bins,
                guide_table,
                block_source.reshape(n_dp, block_source.shape[0] // n_dp),
                queries,
                key_rows,
                value_rows,
                cotangent,
            )
        ),
    )


def chosen(*arrays):
    n_dp, n_sp = lax.axis_size("dp"), lax.axis_size("sp")
    tok = arrays[0].shape[0]
    block_rows = tok // (n_dp * n_sp)
    if (n_sp * block_rows) % 16 == 0 and HEADS % n_sp == 0:
        return place_outputs(fused(n_dp, n_sp, *arrays))
    return per_device(*arrays)


def solution(mesh):
    placed = (
        P(("dp", "sp"), None),
        P(("dp", "sp"), None),
        P(("dp", "sp"), None),
        P(("dp", "sp"), None),
        P(),
        P(),
        P(),
        P(),
        P(),
    )
    return jax.shard_map(
        chosen,
        mesh=mesh,
        in_specs=placed,
        out_specs=(
            P(("dp", "sp"), None),
            P(("dp", "sp"), None),
            P(("dp", "sp"), None),
            P(("dp", "sp"), None),
        ),
        check_vma=False,
    )
```
